256 devices in a mesh: seq: 32 (over x_lo, z, core), head: 8 (over y, x_hi).
Axes of the slice: x: 4 (x_hi: 2, x_lo: 2; x = x_hi * 2 + x_lo), y: 4, z: 8, core: 2. Of those that a mesh axis runs over, the one named last changes fastest.
Arguments:
- queries: bfloat16 [16384, 4096], P(('seq', 'head')), may hold values from -12.75 to 12.75
- keys: bfloat16 [16384, 1024], P(('seq', 'head')), may hold values from -9 to 9
- values: bfloat16 [16384, 1024], P(('seq', 'head')), may hold values from -6 to 6
- output_gradient: bfloat16 [16384, 4096], P(('seq', 'head')), may hold values from -6 to 6
- outputs: bfloat16 [16384, 4096], P(('seq', 'head')), may hold values from -2 to 2
- block_order: int32 [64], replicated, may hold values from 0 to 63, as said below
- doc_start: int32 [64], replicated, may hold values 0 or 1
Outputs:
- grad_queries: bfloat16 [16384, 4096], P(('seq', 'head'))
- key_gradients: bfloat16 [16384, 1024], P(('seq', 'head'))
- value_gradients: bfloat16 [16384, 1024], P(('seq', 'head'))
The draws below stay inside these ranges and needn't reach their ends.
Inputs may be any that keep to these rules, and one draw needn't show every extreme that they name: `block_order`: for one c and every slab s, slots 2 s and 2 s + 1 hold, in either order, blocks b and 63 - b with b = (s + c) mod 32.
All inputs are finite; a program needn't handle non-finite values.
Results may differ from the reference program's by a relative error of at most 0.007.
Values may be sent and summed in bfloat16 or wider, within the bound.
No kernel may reach another device: no remote copies, remote signals or barrier semaphores. Data moves between devices by JAX's collectives and lax.ppermute only.
A program may use at most 128 MiB of HBM per device.

```python
import math
import jax
import jax.numpy as jnp
from jax import lax

QUERY_HEADS = 32
KEY_VALUE_HEADS = 8
HEAD_DIMENSION = 128
SLAB_ROWS = 512
BLK = 256
NBLK = 64
SLAB_REACH = 2
SEQUENCE_TOKENS = 16384
N_SEQ = 32


def scale_per_row(key, heads):
    return jnp.exp(jax.random.uniform(key, (SEQUENCE_TOKENS, heads, 1), jnp.float32, math.log(0.3), math.log(3.0)))


def draw_keys(key, part):
    key = jax.random.fold_in(key, 3)
    scale_random_key, value_random_key = jax.random.split(key)
    scale_factors = scale_per_row(scale_random_key, KEY_VALUE_HEADS)
    unscaled_values = jnp.clip(jax.random.normal(value_random_key, (SEQUENCE_TOKENS, KEY_VALUE_HEADS, HEAD_DIMENSION), jnp.float32), -3.0, 3.0) * scale_factors
    return unscaled_values.reshape(SEQUENCE_TOKENS, KEY_VALUE_HEADS * HEAD_DIMENSION).astype(jnp.bfloat16)


def draw_queries(key, part):
    key = jax.random.fold_in(key, 5)
    scale_random_key, value_random_key = jax.random.split(key)
    scale_factors = scale_per_row(scale_random_key, QUERY_HEADS)
    unscaled_values = jnp.clip(jax.random.normal(value_random_key, (SEQUENCE_TOKENS, QUERY_HEADS, HEAD_DIMENSION), jnp.float32), -4.0, 4.0) * scale_factors
    return unscaled_values.reshape(SEQUENCE_TOKENS, QUERY_HEADS * HEAD_DIMENSION).astype(jnp.bfloat16)


def draw_block_order(key, part):
    key = jax.random.fold_in(key, 7)
    first_key, second_random_key = jax.random.split(key)
    rotation = jax.random.randint(first_key, (), 0, N_SEQ)
    leading = (jnp.arange(N_SEQ, dtype=jnp.int32) + rotation) % N_SEQ
    flips = jax.random.randint(second_random_key, (N_SEQ,), 0, 2)
    first = jnp.where(flips == 1, 2 * N_SEQ - 1 - leading, leading)
    return jnp.stack([first, 2 * N_SEQ - 1 - first], axis=1).reshape(NBLK).astype(jnp.int32)


def with_ends(drawn, stream_key, least, largest):
    longest = drawn.shape.index(max(drawn.shape))
    spots = []
    for shift in (0, 1):
        where = [jax.random.randint(jax.random.fold_in(stream_key, axis), (), 0, length) for axis, length in enumerate(drawn.shape)]
        where[longest] = (where[longest] + shift) % drawn.shape[longest]
        spots.append(tuple(where))
    return drawn.at[spots[0]].set(least).at[spots[1]].set(largest)


def block_levels(stream_key, extent, shards, smallest, top_value):
    def one(position, shards_of):
        draws = jax.random.uniform(jax.random.fold_in(jax.random.fold_in(stream_key, 6), position), (shards_of,), jnp.float32, smallest / len(shards), top_value / len(shards))
        return jnp.repeat(jnp.exp(draws), extent[position] // shards_of).reshape((-1,) + (1,) * (len(extent) - position - 1))

    level = one(*shards[0])
    for cut in shards[1:]:
        level = level * one(*cut)
    return level


def normal_values(key, shape, spread, most, cuts=(), kind=jnp.bfloat16):
    gain = block_levels(key, shape, cuts, -0.22, 0.18) if cuts else 1.0
    result = jax.random.normal(key, shape, jnp.float32) * spread * gain
    return jnp.minimum(jnp.maximum(result, -most), most).astype(kind)


def setup_inputs(seed: int = 0) -> dict:
    streams_of = jax.random.split(jax.random.key(seed), 8)
    queries = draw_queries(jax.random.fold_in(streams_of[7], 71), 0)
    keys = draw_keys(jax.random.fold_in(streams_of[7], 71), 0)
    values = normal_values(streams_of[2], (SEQUENCE_TOKENS, KEY_VALUE_HEADS * HEAD_DIMENSION), 1.0, 6.0, ((0, 256),))
    output_gradient = normal_values(streams_of[3], (SEQUENCE_TOKENS, QUERY_HEADS * HEAD_DIMENSION), 1.0, 6.0, ((0, 256),))
    outputs = normal_values(streams_of[4], (SEQUENCE_TOKENS, QUERY_HEADS * HEAD_DIMENSION), 0.3, 2.0, ((0, 256),))
    block_order = draw_block_order(jax.random.fold_in(streams_of[7], 71), 0)
    doc_start = with_ends((jax.random.randint(streams_of[6], (NBLK,), 0, 8) < 1).astype(jnp.int32), jax.random.fold_in(streams_of[6], 1), 0, 1)
    return {"queries": queries, "keys": keys, "values": values, "output_gradient": output_gradient, "outputs": outputs, "block_order": block_order, "doc_start": doc_start}


def layout_positions(block_order, doc_start):
    starts = jnp.where(jnp.arange(NBLK) > 0, doc_start, 0).astype(jnp.int32)
    documents = jnp.cumsum(starts).astype(jnp.int32)
    row_index = jnp.arange(SEQUENCE_TOKENS, dtype=jnp.int32)
    blocks = jnp.take(block_order, row_index // BLK).astype(jnp.int32)
    positions = (blocks * BLK + row_index % BLK).astype(jnp.int32)
    row_docs = jnp.take(documents, blocks).astype(jnp.int32)
    return (positions, row_docs)

def reference(queries, keys, values, output_gradient, outputs, block_order, doc_start):
    query_groups = QUERY_HEADS // KEY_VALUE_HEADS
    factor = 1.0 / math.sqrt(HEAD_DIMENSION)
    window_width = (2 * SLAB_REACH + 1) * SLAB_ROWS
    positions, row_docs = layout_positions(block_order, doc_start)
    slabs_of_keys = keys.astype(jnp.float32).reshape(N_SEQ, SLAB_ROWS, KEY_VALUE_HEADS, HEAD_DIMENSION)
    slabs_of_values = values.astype(jnp.float32).reshape(N_SEQ, SLAB_ROWS, KEY_VALUE_HEADS, HEAD_DIMENSION)
    pos_slabs = positions.reshape(N_SEQ, SLAB_ROWS)
    doc_slabs = row_docs.reshape(N_SEQ, SLAB_ROWS)
    slabs_of_queries = queries.reshape(N_SEQ, SLAB_ROWS, KEY_VALUE_HEADS, query_groups, HEAD_DIMENSION)
    gradient_slabs = output_gradient.reshape(N_SEQ, SLAB_ROWS, KEY_VALUE_HEADS, query_groups, HEAD_DIMENSION)
    output_slabs = outputs.reshape(N_SEQ, SLAB_ROWS, KEY_VALUE_HEADS, query_groups, HEAD_DIMENSION)
    offsets = jnp.arange(-SLAB_REACH, SLAB_REACH + 1, dtype=jnp.int32)

    def slab(carry, inputs):
        key_gradient, value_gradient = carry
        query_slab, grad_slab, out_slab, slab_pos, slab_doc, index = inputs
        slab_window = ((index + offsets) % N_SEQ).astype(jnp.int32)
        every_key = jnp.take(slabs_of_keys, slab_window, axis=0).reshape(window_width, KEY_VALUE_HEADS, HEAD_DIMENSION)
        every_value = jnp.take(slabs_of_values, slab_window, axis=0).reshape(window_width, KEY_VALUE_HEADS, HEAD_DIMENSION)
        key_pos = jnp.take(pos_slabs, slab_window, axis=0).reshape(window_width)
        key_doc = jnp.take(doc_slabs, slab_window, axis=0).reshape(window_width)
        query_float = query_slab.astype(jnp.float32)
        gradient_float = grad_slab.astype(jnp.float32)
        out_f = out_slab.astype(jnp.float32)
        allowed = (key_doc[None, :] == slab_doc[:, None]) & (key_pos[None, :] <= slab_pos[:, None])
        scores = jnp.einsum('rkgd,nkd->kgrn', query_float, every_key) * factor
        scores = jnp.where(allowed, scores, -jnp.inf)
        lse = jax.nn.logsumexp(scores, axis=-1, keepdims=True)
        probs = jnp.exp(scores - lse)
        dprobs = jnp.einsum('rkgd,nkd->kgrn', gradient_float, every_value)
        delta = jnp.transpose(lax.optimization_barrier(jnp.sum(gradient_float * out_f, axis=-1)), (1, 2, 0))[..., None]
        score_gradient = (factor * probs * (dprobs - delta)).astype(jnp.bfloat16).astype(jnp.float32)
        probability_bfloat = probs.astype(jnp.bfloat16).astype(jnp.float32)
        grad_q = jnp.einsum('kgrn,nkd->rkgd', score_gradient, every_key)
        partial_key = jnp.einsum('jmac,ajmv->cjv', score_gradient, query_float).reshape(2 * SLAB_REACH + 1, SLAB_ROWS, KEY_VALUE_HEADS, HEAD_DIMENSION)
        partial_value = jnp.einsum('jmac,ajmv->cjv', probability_bfloat, gradient_float).reshape(2 * SLAB_REACH + 1, SLAB_ROWS, KEY_VALUE_HEADS, HEAD_DIMENSION)
        key_gradient = key_gradient.at[slab_window].add(partial_key)
        value_gradient = value_gradient.at[slab_window].add(partial_value)
        return ((key_gradient, value_gradient), grad_q.astype(jnp.bfloat16).reshape(SLAB_ROWS, QUERY_HEADS * HEAD_DIMENSION))
    window_start = (jnp.zeros((N_SEQ, SLAB_ROWS, KEY_VALUE_HEADS, HEAD_DIMENSION), jnp.float32), jnp.zeros((N_SEQ, SLAB_ROWS, KEY_VALUE_HEADS, HEAD_DIMENSION), jnp.float32))
    inputs = (slabs_of_queries, gradient_slabs, output_slabs, pos_slabs, doc_slabs, jnp.arange(N_SEQ, dtype=jnp.int32))
    (key_gradient, value_gradient), grad_q = lax.scan(slab, window_start, inputs)
    grad_queries = grad_q.reshape(SEQUENCE_TOKENS, QUERY_HEADS * HEAD_DIMENSION)
    key_gradients = key_gradient.astype(jnp.bfloat16).reshape(SEQUENCE_TOKENS, KEY_VALUE_HEADS * HEAD_DIMENSION)
    value_gradients = value_gradient.astype(jnp.bfloat16).reshape(SEQUENCE_TOKENS, KEY_VALUE_HEADS * HEAD_DIMENSION)
    return (grad_queries, key_gradients, value_gradients)
```

```python
import functools
import math

import jax
import jax.numpy as jnp
from jax import lax
from jax.experimental import pallas as pl
from jax.experimental.pallas import tpu as pltpu
from jax.sharding import PartitionSpec as P

QUERY_HEADS = 32
KEY_VALUE_HEADS = 8
GROUP = QUERY_HEADS // KEY_VALUE_HEADS
HEAD = 128
REACH = 2
WINDOW = 2 * REACH + 1
BLK = 256
SCALE = 1.0 / math.sqrt(HEAD)
SCALE2 = SCALE * math.log2(math.e)
MASKED = -1e30
DELTA_ROWS = 16


def send(value, steps):
    count = lax.axis_size("seq")
    return lax.ppermute(value, "seq", [(i, (i + steps) % count) for i in range(count)])


def swap_heads(value):
    return lax.all_to_all(value, "head", split_axis=0, concat_axis=0, tiled=True)


def pack_kernel(owners, q_ref, g_ref, o_ref, k_ref, v_ref, kv_ref, qg_ref):
    rows = q_ref.shape[0]
    width = GROUP * HEAD
    for n in range(owners):
        kv_ref[n, :, :HEAD] = k_ref[:, n * HEAD : (n + 1) * HEAD]
        kv_ref[n, :, HEAD:] = v_ref[:, n * HEAD : (n + 1) * HEAD]
        deltas = []
        for h in range(GROUP):
            cols = slice(n * width + h * HEAD, n * width + (h + 1) * HEAD)
            grad = g_ref[:, cols]
            qg_ref[n, h * rows : (h + 1) * rows, :] = q_ref[:, cols]
            qg_ref[n, (GROUP + h) * rows : (GROUP + h + 1) * rows, :] = grad
            deltas.append(grad.astype(jnp.float32) * o_ref[:, cols].astype(jnp.float32))
        lines = []
        for h in range(0, GROUP, 2):
            both = jnp.concatenate(deltas[h : h + 2], axis=0)
            lines.append(jnp.sum(both.T, axis=0, keepdims=True))
        delta = jnp.concatenate(lines, axis=0)
        high = delta.astype(jnp.bfloat16).astype(jnp.float32)
        spare = jnp.zeros((DELTA_ROWS - 2 * GROUP // 2, HEAD), jnp.float32)
        tile = jnp.concatenate([high, delta - high, spare], axis=0)
        qg_ref[n, 2 * GROUP * rows :, :] = tile.astype(jnp.bfloat16)


def pack(queries, keys, values, grads, outputs, heads):
    rows = queries.shape[0]
    owners = 2
    wide = pl.BlockSpec((rows, owners * GROUP * HEAD), lambda n: (0, n))
    narrow = pl.BlockSpec((rows, owners * HEAD), lambda n: (0, n))
    qg_rows = 2 * GROUP * rows + DELTA_ROWS
    return pl.pallas_call(
        functools.partial(pack_kernel, owners),
        grid=(heads // owners,),
        in_specs=[wide, wide, wide, narrow, narrow],
        out_specs=[
            pl.BlockSpec((owners, rows, 2 * HEAD), lambda n: (n, 0, 0)),
            pl.BlockSpec((owners, qg_rows, HEAD), lambda n: (n, 0, 0)),
        ],
        out_shape=[
            jax.ShapeDtypeStruct((heads, rows, 2 * HEAD), jnp.bfloat16),
            jax.ShapeDtypeStruct((heads, qg_rows, HEAD), jnp.bfloat16),
        ],
        name="pack",
    )(queries, grads, outputs, keys, values)


def attention_kernel(
    seq_size, mine_ref, order_ref, start_ref, qg_ref, *refs
):
    kv_refs = refs[:WINDOW]
    dq_ref = refs[WINDOW]
    dkv_refs = refs[WINDOW + 1 : 2 * WINDOW + 1]
    docs_ref, keep_ref, kv, scores, qt, gt, dqt, dkv, stats, sems = refs[2 * WINDOW + 1 :]
    sources = qg_ref.shape[0]
    rows = (qg_ref.shape[1] - DELTA_ROWS) // (2 * GROUP)
    chunk = GROUP * rows
    per_block = BLK // rows
    slots = 2 * WINDOW
    own = 2 * REACH

    copies = [
        pltpu.make_async_copy(kv_refs[n], kv.at[pl.ds(n * 2 * BLK, 2 * BLK)], sems.at[n])
        for n in range(WINDOW)
    ]
    for copy in copies:
        copy.start()

    def count(b, running):
        running = running + jnp.where(b > 0, start_ref[b], 0)
        docs_ref[b] = running
        return running

    lax.fori_loop(0, order_ref.shape[0], count, jnp.int32(0))
    mine = mine_ref[0]
    blocks = []
    for j in range(slots):
        slab = lax.rem(mine + (j // 2 - REACH) + seq_size, seq_size)
        blocks.append(order_ref[2 * slab + j % 2])
    for i in range(2):
        for j in range(slots):
            kept = (blocks[j] <= blocks[own + i]) & (docs_ref[blocks[j]] == docs_ref[blocks[own + i]])
            keep_ref[i * slots + j] = kept.astype(jnp.int32)

    for i in range(2):
        for c in range(per_block):
            source = i * per_block + c
            qt[i, :, c * chunk : (c + 1) * chunk] = qg_ref[source, :chunk, :].T
            gt[i, :, c * chunk : (c + 1) * chunk] = qg_ref[source, chunk : 2 * chunk, :].T
    dkv[...] = jnp.zeros_like(dkv)
    for copy in copies:
        copy.wait()

    def keys_of(j):
        return kv[pl.ds(pl.multiple_of(j * BLK, BLK), BLK), :HEAD]

    def values_of(j):
        return kv[pl.ds(pl.multiple_of(j * BLK, BLK), BLK), HEAD:]

    def score(i, j, diagonal):
        keys = keys_of(j)
        for c in range(per_block):
            lanes = slice(c * chunk, (c + 1) * chunk)
            s = jnp.dot(keys, qt[i, :, lanes], preferred_element_type=jnp.float32)
            if diagonal:
                key_at = lax.broadcasted_iota(jnp.int32, (BLK, chunk), 0)
                query_at = c * rows + lax.broadcasted_iota(jnp.int32, (BLK, chunk), 1) % rows
                s = jnp.where(key_at <= query_at, s, MASKED)
            scores[j, :, lanes] = s
            top = jnp.max(s, axis=0, keepdims=True)
            if diagonal:
                stats[0:1, lanes] = top
                stats[1:2, lanes] = jnp.sum(jnp.exp2((s - top) * SCALE2), axis=0, keepdims=True)
            else:
                before = stats[0:1, lanes]
                top = jnp.maximum(top, before)
                stats[0:1, lanes] = top
                stats[1:2, lanes] = stats[1:2, lanes] * jnp.exp2((before - top) * SCALE2) + jnp.sum(
                    jnp.exp2((s - top) * SCALE2), axis=0, keepdims=True
                )

    def gradients(i, j, first):
        keys = keys_of(j)
        values = values_of(j)
        add_k = None
        add_v = None
        for c in range(per_block):
            source = i * per_block + c
            lanes = slice(c * chunk, (c + 1) * chunk)
            probs = jnp.exp2(scores[j, :, lanes] * SCALE2 - stats[2:3, lanes])
            dprobs = jnp.dot(values, gt[i, :, lanes], preferred_element_type=jnp.float32)
            dscores = ((SCALE * probs) * (dprobs - stats[3:4, lanes])).astype(jnp.bfloat16)
            probs = probs.astype(jnp.bfloat16)
            v = jnp.dot(probs, qg_ref[source, chunk : 2 * chunk, :], preferred_element_type=jnp.float32)
            k = jnp.dot(dscores, qg_ref[source, :chunk, :], preferred_element_type=jnp.float32)
            add_v = v if add_v is None else add_v + v
            add_k = k if add_k is None else add_k + k
            q = lax.dot_general(
                keys, dscores, (((0,), (0,)), ((), ())), preferred_element_type=jnp.float32
            )
            dqt[:, lanes] = q if first else dqt[:, lanes] + q
        here = pl.ds(pl.multiple_of(j * BLK, BLK), BLK)
        dkv[here, :HEAD] += add_k
        dkv[here, HEAD:] += add_v

    for i in range(2):
        for c in range(per_block):
            base = 2 * chunk
            source = i * per_block + c
            tile = qg_ref[source, base:, :].astype(jnp.float32)
            delta = tile[0:2, :] + tile[2:4, :]
            stats[3:4, c * chunk : c * chunk + HEAD] = delta[0:1, :]
            stats[3:4, c * chunk + HEAD : (c + 1) * chunk] = delta[1:2, :]
        score(i, own + i, True)

        def visit_scores(j, _):
            @pl.when((keep_ref[i * slots + j] == 1) & (j != own + i))
            def _():
                score(i, j, False)

            return 0

        lax.fori_loop(0, slots, visit_scores, 0)
        stats[2:3, :] = stats[0:1, :] * SCALE2 + jnp.log2(stats[1:2, :])
        gradients(i, own + i, True)

        def visit_gradients(j, _):
            @pl.when((keep_ref[i * slots + j] == 1) & (j != own + i))
            def _():
                gradients(i, j, False)

            return 0

        lax.fori_loop(0, slots, visit_gradients, 0)
        for c in range(per_block):
            dq_ref[i * per_block + c] = dqt[:, c * chunk : (c + 1) * chunk].T.astype(jnp.bfloat16)

    for n in range(WINDOW):
        dkv_refs[n][...] = dkv[n * 2 * BLK : (n + 1) * 2 * BLK, :].astype(dkv_refs[n].dtype)


def attention(mine, block_order, doc_start, qg, kvs, seq_size):
    sources, qg_rows, _ = qg.shape
    rows = (qg_rows - DELTA_ROWS) // (2 * GROUP)
    slab = sources * rows
    lanes = BLK * GROUP
    smem = pl.BlockSpec(memory_space=pltpu.SMEM)
    vmem = pl.BlockSpec(memory_space=pltpu.VMEM)
    return pl.pallas_call(
        functools.partial(attention_kernel, seq_size),
        in_specs=[smem, smem, smem, vmem] + [pl.BlockSpec(memory_space=pl.ANY)] * WINDOW,
        out_specs=[vmem] * (1 + WINDOW),
        out_shape=[jax.ShapeDtypeStruct((sources, GROUP * rows, HEAD), jnp.bfloat16)]
        + [
            jax.ShapeDtypeStruct((slab, 2 * HEAD), jnp.float32 if n == REACH else jnp.bfloat16)
            for n in range(WINDOW)
        ],
        scratch_shapes=[
            pltpu.SMEM((block_order.shape[0],), jnp.int32),
            pltpu.SMEM((4 * WINDOW,), jnp.int32),
            pltpu.VMEM((WINDOW * slab, 2 * HEAD), jnp.bfloat16),
            pltpu.VMEM((2 * WINDOW, BLK, lanes), jnp.float32),
            pltpu.VMEM((2, HEAD, lanes), jnp.bfloat16),
            pltpu.VMEM((2, HEAD, lanes), jnp.bfloat16),
            pltpu.VMEM((HEAD, lanes), jnp.float32),
            pltpu.VMEM((WINDOW * slab, 2 * HEAD), jnp.float32),
            pltpu.VMEM((8, lanes), jnp.float32),
            pltpu.SemaphoreType.DMA((WINDOW,)),
        ],
        compiler_params=pltpu.CompilerParams(vmem_limit_bytes=40 * 1024 * 1024),
        cost_estimate=pl.CostEstimate(flops=3_000_000_000, bytes_accessed=4_000_000, transcendentals=8_000_000),
        name="attention",
    )(mine, block_order, doc_start, qg, *kvs)


def local(queries, keys, values, output_gradient, outputs, block_order, doc_start):
    heads = lax.axis_size("head")
    seq_size = lax.axis_size("seq")
    rows = queries.shape[0]
    kv, qg = pack(queries, keys, values, output_gradient, outputs, heads)
    kv = swap_heads(kv).reshape(heads * rows, 2 * HEAD)
    qg = swap_heads(qg)
    kvs = [kv if n == REACH else send(kv, REACH - n) for n in range(WINDOW)]
    mine = lax.axis_index("seq").astype(jnp.int32).reshape(1)
    dq, *dkvs = attention(mine, block_order, doc_start, qg, kvs, seq_size)
    total = dkvs[REACH]
    for n in range(WINDOW):
        if n != REACH:
            total = total + send(dkvs[n], n - REACH).astype(jnp.float32)
    dq = swap_heads(dq)
    dkv = swap_heads(total.astype(jnp.bfloat16).reshape(heads, rows, 2 * HEAD))
    dq = dq.reshape(heads, GROUP, rows, HEAD).transpose(2, 0, 1, 3).reshape(rows, heads * GROUP * HEAD)
    dk = dkv[:, :, :HEAD].transpose(1, 0, 2).reshape(rows, heads * HEAD)
    dv = dkv[:, :, HEAD:].transpose(1, 0, 2).reshape(rows, heads * HEAD)
    return dq, dk, dv


def solution(mesh):
    rows = P(("seq", "head"), None)
    return jax.shard_map(
        local,
        mesh=mesh,
        in_specs=(rows, rows, rows, rows, rows, P(), P()),
        out_specs=(rows, rows, rows),
        check_vma=False,
    )
```

```python
import functools
import math

import jax
import jax.numpy as jnp
from jax import lax
from jax.experimental import pallas as pl
from jax.experimental.pallas import tpu as pltpu
from jax.sharding import PartitionSpec as P

QUERY_HEADS = 32
KEY_VALUE_HEADS = 8
GROUP = QUERY_HEADS // KEY_VALUE_HEADS
HEAD = 128
REACH = 2
BLK = 256
SCALE = 1.0 / math.sqrt(HEAD)
SCALE2 = SCALE * math.log2(math.e)
MASKED = -1e30
DELTA_ROWS = 16
MIB = 1024 * 1024
NEAR = 4
BLOCKS = 10


def send(value, steps):
    count = lax.axis_size("seq")
    return lax.ppermute(value, "seq", [(i, (i + steps) % count) for i in range(count)])


def swap_pair(value):
    count = lax.axis_size("seq")
    return lax.ppermute(value, "seq", [(i, i ^ 1) for i in range(count)])


def swap_cross(value):
    count = lax.axis_size("seq")
    return lax.ppermute(value, "seq", [(i, (i + (1 if i % 2 else count - 1)) % count) for i in range(count)])


def swap_heads(value):
    return lax.all_to_all(value, "head", split_axis=0, concat_axis=0, tiled=True)


def near_array(shape, dtype):
    return pltpu.VMEM(shape, dtype)


def near(value):
    return pltpu.with_memory_space_constraint(value, pltpu.VMEM)


SMEM = pl.BlockSpec(memory_space=pltpu.SMEM)
VMEM = pl.BlockSpec(memory_space=pltpu.VMEM)


def pack_kernel(owners, q_ref, g_ref, o_ref, k_ref, v_ref, out_ref):
    rows = q_ref.shape[0]
    width = GROUP * HEAD
    base = 2 * GROUP * rows
    for n in range(owners):
        deltas = []
        for h in range(GROUP):
            cols = slice(n * width + h * HEAD, n * width + (h + 1) * HEAD)
            grad = g_ref[:, cols]
            out_ref[n, h * rows : (h + 1) * rows, :] = q_ref[:, cols]
            out_ref[n, (GROUP + h) * rows : (GROUP + h + 1) * rows, :] = grad
            deltas.append(grad.astype(jnp.float32) * o_ref[:, cols].astype(jnp.float32))
        lines = []
        for h in range(0, GROUP, 2):
            both = jnp.concatenate(deltas[h : h + 2], axis=0)
            lines.append(jnp.sum(both.T, axis=0, keepdims=True))
        delta = jnp.concatenate(lines, axis=0)
        high = delta.astype(jnp.bfloat16).astype(jnp.float32)
        spare = jnp.zeros((DELTA_ROWS - GROUP, HEAD), jnp.float32)
        tile = jnp.concatenate([high, delta - high, spare], axis=0)
        out_ref[n, base : base + DELTA_ROWS, :] = tile.astype(jnp.bfloat16)
        out_ref[n, base + DELTA_ROWS : base + DELTA_ROWS + rows, :] = k_ref[:, n * HEAD : (n + 1) * HEAD]
        out_ref[n, base + DELTA_ROWS + rows :, :] = v_ref[:, n * HEAD : (n + 1) * HEAD]


def pack(queries, keys, values, grads, outputs, heads):
    rows = queries.shape[0]
    owners = 2
    wide = pl.BlockSpec((rows, owners * GROUP * HEAD), lambda n: (0, n))
    narrow = pl.BlockSpec((rows, owners * HEAD), lambda n: (0, n))
    out_rows = (2 * GROUP + 2) * rows + DELTA_ROWS
    return pl.pallas_call(
        functools.partial(pack_kernel, owners),
        grid=(heads // owners,),
        in_specs=[wide, wide, wide, narrow, narrow],
        out_specs=pl.BlockSpec((owners, out_rows, HEAD), lambda n: (n, 0, 0)),
        out_shape=jax.ShapeDtypeStruct((heads, out_rows, HEAD), jnp.bfloat16),
        name="pack",
    )(queries, grads, outputs, keys, values)


def plan_kernel(seq_size, mine_ref, order_ref, start_ref, keep_ref, docs_ref):
    def count(b, running):
        running = running + jnp.where(b > 0, start_ref[b], 0)
        docs_ref[b] = running
        return running

    lax.fori_loop(0, order_ref.shape[0], count, jnp.int32(0))
    mine = mine_ref[0]
    odd = lax.rem(mine, 2)
    steps = (0, 1 - 2 * odd, -REACH, REACH, 2 * odd - 1)
    blocks = []
    for step in steps:
        slab = lax.rem(mine + step + seq_size, seq_size)
        blocks += [order_ref[2 * slab], order_ref[2 * slab + 1]]
    docs = [docs_ref[b] for b in blocks]
    for i in range(2):
        for j in range(BLOCKS):
            kept = (blocks[j] <= blocks[i]) & (docs[j] == docs[i])
            keep_ref[i * BLOCKS + j] = kept.astype(jnp.int32)


def plan(mine, block_order, doc_start, seq_size):
    return pl.pallas_call(
        functools.partial(plan_kernel, seq_size),
        in_specs=[SMEM] * 3,
        out_specs=SMEM,
        out_shape=jax.ShapeDtypeStruct((2 * BLOCKS,), jnp.int32),
        scratch_shapes=[pltpu.SMEM((block_order.shape[0],), jnp.int32)],
        name="plan",
    )(mine, block_order, doc_start)


def block_of(ref, j, first, rows):
    per_block = BLK // rows
    tiles = ref[pl.ds(j * per_block, per_block), first : first + rows, :]
    return tiles.reshape(BLK, HEAD)


def near_kernel(rows, keep_ref, got_ref, pair_ref, e_ref, d_ref, qt_ref, gt_ref, u_ref, stat_ref, kv, scores):
    per_block = BLK // rows
    chunk = GROUP * rows
    sources = 2 * per_block
    kv_at = 2 * chunk + DELTA_ROWS
    kv[:sources] = got_ref[:, kv_at:, :]
    kv[sources:] = pair_ref[...]

    def score(i, j, diagonal):
        keys = block_of(kv, j, 0, rows)
        for c in range(per_block):
            lanes = slice(c * chunk, (c + 1) * chunk)
            s = jnp.dot(keys, qt_ref[i, :, lanes], preferred_element_type=jnp.float32)
            if diagonal:
                key_at = lax.broadcasted_iota(jnp.int32, (BLK, chunk), 0)
                query_at = c * rows + lax.broadcasted_iota(jnp.int32, (BLK, chunk), 1) % rows
                s = jnp.where(key_at <= query_at, s, MASKED)
            scores[j, :, lanes] = s
            top = jnp.max(s, axis=0, keepdims=True)
            stat_ref[i, 0:1, lanes] = top if diagonal else jnp.maximum(top, stat_ref[i, 0:1, lanes])

    def weigh(i, j, first):
        keys_t = block_of(kv, j, 0, rows).T
        values = block_of(kv, j, rows, rows)
        parts = []
        for c in range(per_block):
            lanes = slice(c * chunk, (c + 1) * chunk)
            e = jnp.exp2((scores[j, :, lanes] - stat_ref[i, 0:1, lanes]) * SCALE2)
            total = jnp.sum(e, axis=0, keepdims=True)
            stat_ref[i, 1:2, lanes] = total if first else stat_ref[i, 1:2, lanes] + total
            dprobs = jnp.dot(values, gt_ref[i, :, lanes], preferred_element_type=jnp.float32)
            d = (e * (dprobs - stat_ref[i, 2:3, lanes])).astype(jnp.bfloat16)
            e_ref[i * NEAR + j, :, lanes] = e.astype(jnp.bfloat16)
            d_ref[i * NEAR + j, :, lanes] = d
            parts.append(d)
        u = jnp.dot(keys_t, jnp.concatenate(parts, axis=1), preferred_element_type=jnp.float32)
        u_ref[i] = u if first else u_ref[i] + u

    for i in range(2):
        for c in range(per_block):
            source = i * per_block + c
            lanes = slice(c * chunk, (c + 1) * chunk)
            qt_ref[i, :, lanes] = got_ref[source, :chunk, :].T
            gt_ref[i, :, lanes] = got_ref[source, chunk : 2 * chunk, :].T
            tile = got_ref[source, 2 * chunk : kv_at, :].astype(jnp.float32)
            delta = tile[0:2, :] + tile[2:4, :]
            stat_ref[i, 2:3, c * chunk : c * chunk + HEAD] = delta[0:1, :]
            stat_ref[i, 2:3, c * chunk + HEAD : (c + 1) * chunk] = delta[1:2, :]
        score(i, i, True)

        def visit_scores(j, _):
            @pl.when((keep_ref[i * BLOCKS + j] == 1) & (j != i))
            def _():
                score(i, j, False)

            return 0

        lax.fori_loop(0, NEAR, visit_scores, 0)
        weigh(i, i, True)

        def visit_weights(j, _):
            @pl.when((keep_ref[i * BLOCKS + j] == 1) & (j != i))
            def _():
                weigh(i, j, False)

            return 0

        lax.fori_loop(0, NEAR, visit_weights, 0)


def near_part(keep, got, pair, rows):
    lanes = BLK * GROUP
    return pl.pallas_call(
        functools.partial(near_kernel, rows),
        in_specs=[SMEM, VMEM, VMEM],
        out_specs=[VMEM] * 6,
        out_shape=[
            near_array((2 * NEAR, BLK, lanes), jnp.bfloat16),
            near_array((2 * NEAR, BLK, lanes), jnp.bfloat16),
            near_array((2, HEAD, lanes), jnp.bfloat16),
            near_array((2, HEAD, lanes), jnp.bfloat16),
            near_array((2, HEAD, lanes), jnp.float32),
            near_array((2, 8, lanes), jnp.float32),
        ],
        scratch_shapes=[
            pltpu.VMEM((2 * pair.shape[0],) + pair.shape[1:], jnp.bfloat16),
            pltpu.VMEM((NEAR, BLK, lanes), jnp.float32),
        ],
        compiler_params=pltpu.CompilerParams(vmem_limit_bytes=24 * MIB),
        cost_estimate=pl.CostEstimate(flops=3_000_000_000, bytes_accessed=4_000_000, transcendentals=8_000_000),
        name="near_part",
    )(keep, got, pair)


def far_kernel(
    rows, keep_ref, got_ref, before_ref, after_ref, cross_ref, e_ref, d_ref, qt_ref, gt_ref, u_ref,
    stat_ref, to_before, to_after, to_cross, to_pair, out_ref, own_ref, kv, scores, acc, stats, dqt_ref, alpha_ref,
):
    per_block = BLK // rows
    chunk = GROUP * rows
    sources = 2 * per_block
    far_blocks = BLOCKS - NEAR
    kv[:sources] = before_ref[...]
    kv[sources : 2 * sources] = after_ref[...]

    kv[2 * sources :] = cross_ref[...]
    acc[...] = jnp.zeros_like(acc)

    def score(i, j):
        keys = block_of(kv, j, 0, rows)
        for c in range(per_block):
            lanes = slice(c * chunk, (c + 1) * chunk)
            s = jnp.dot(keys, qt_ref[i, :, lanes], preferred_element_type=jnp.float32)
            scores[j, :, lanes] = s
            before = stats[0:1, lanes]
            top = jnp.maximum(jnp.max(s, axis=0, keepdims=True), before)
            stats[0:1, lanes] = top
            stats[1:2, lanes] = stats[1:2, lanes] * jnp.exp2((before - top) * SCALE2) + jnp.sum(
                jnp.exp2((s - top) * SCALE2), axis=0, keepdims=True
            )

    def queries_of(i, first):
        tiles = got_ref[i * per_block : (i + 1) * per_block, first : first + chunk, :]
        return tiles.reshape(per_block * chunk, HEAD)

    def add(j, k, v):
        here = pl.ds(j * per_block, per_block)
        acc[here, :rows, :] += k.reshape(per_block, rows, HEAD)
        acc[here, rows:, :] += v.reshape(per_block, rows, HEAD)

    def gradients(i, j):
        keys_t = block_of(kv, j, 0, rows).T
        values = block_of(kv, j, rows, rows)
        all_p, all_d = [], []
        for c in range(per_block):
            lanes = slice(c * chunk, (c + 1) * chunk)
            probs = jnp.exp2(scores[j, :, lanes] * SCALE2 - stats[2:3, lanes])
            dprobs = jnp.dot(values, gt_ref[i, :, lanes], preferred_element_type=jnp.float32)
            all_d.append(((SCALE * probs) * (dprobs - stat_ref[i, 2:3, lanes])).astype(jnp.bfloat16))
            all_p.append(probs.astype(jnp.bfloat16))
        probs = jnp.concatenate(all_p, axis=1)
        dscores = jnp.concatenate(all_d, axis=1)
        v = jnp.dot(probs, queries_of(i, chunk), preferred_element_type=jnp.float32)
        k = jnp.dot(dscores, queries_of(i, 0), preferred_element_type=jnp.float32)
        dqt_ref[i] += jnp.dot(keys_t, dscores, preferred_element_type=jnp.float32)
        add(j, k, v)

    def pair_gradients(i, j):
        p = (e_ref[i * NEAR + j].astype(jnp.float32) * alpha_ref[i, 0:1, :]).astype(jnp.bfloat16)
        d = (d_ref[i * NEAR + j].astype(jnp.float32) * alpha_ref[i, 1:2, :]).astype(jnp.bfloat16)
        v = jnp.dot(p, queries_of(i, chunk), preferred_element_type=jnp.float32)
        k = jnp.dot(d, queries_of(i, 0), preferred_element_type=jnp.float32)
        add(far_blocks + j, k, v)

    for i in range(2):
        stats[0:2, :] = stat_ref[i, 0:2, :]

        def visit_scores(j, _):
            @pl.when(keep_ref[i * BLOCKS + NEAR + j] == 1)
            def _():
                score(i, j)

            return 0

        lax.fori_loop(0, far_blocks, visit_scores, 0)
        lse = stats[0:1, :] * SCALE2 + jnp.log2(stats[1:2, :])
        stats[2:3, :] = lse
        alpha = jnp.exp2(stat_ref[i, 0:1, :] * SCALE2 - lse)
        alpha_ref[i, 0:1, :] = alpha
        alpha_ref[i, 1:2, :] = alpha * SCALE
        dqt_ref[i] = u_ref[i] * (alpha * SCALE)

        def visit_gradients(j, _):
            @pl.when(keep_ref[i * BLOCKS + NEAR + j] == 1)
            def _():
                gradients(i, j)

            return 0

        lax.fori_loop(0, far_blocks, visit_gradients, 0)

        def visit_pair(j, _):
            @pl.when(keep_ref[i * BLOCKS + j] == 1)
            def _():
                pair_gradients(i, j)

            return 0

        lax.fori_loop(0, NEAR, visit_pair, 0)
        for c in range(per_block):
            dq = dqt_ref[i, :, c * chunk : (c + 1) * chunk].T
            out_ref[i * per_block + c, :chunk, :] = dq.astype(jnp.bfloat16)

    own_ref[...] = acc[3 * sources : 4 * sources]
    for n, ref in enumerate((to_before, to_after, to_cross)):
        ref[...] = acc[n * sources : (n + 1) * sources].astype(jnp.bfloat16)
    to_pair[...] = acc[4 * sources :].astype(jnp.bfloat16)


def far_part(keep, got, before, after, cross, state, rows):
    lanes = BLK * GROUP
    e, d, qt, gt, u, stat = state
    chunk = GROUP * rows
    sources, tall, _ = before.shape
    return pl.pallas_call(
        functools.partial(far_kernel, rows),
        in_specs=[SMEM] + [VMEM] * 10,
        out_specs=[VMEM] * 6,
        out_shape=[
            *[jax.ShapeDtypeStruct((sources, tall, HEAD), jnp.bfloat16)] * 4,
            jax.ShapeDtypeStruct((sources, chunk + tall, HEAD), jnp.bfloat16),
            jax.ShapeDtypeStruct((sources, tall, HEAD), jnp.float32),
        ],
        scratch_shapes=[
            pltpu.VMEM((3 * sources, tall, HEAD), jnp.bfloat16),
            pltpu.VMEM((BLOCKS - NEAR, BLK, lanes), jnp.float32),
            pltpu.VMEM((5 * sources, tall, HEAD), jnp.float32),
            pltpu.VMEM((8, lanes), jnp.float32),
            pltpu.VMEM((2, HEAD, lanes), jnp.float32),
            pltpu.VMEM((2, 8, lanes), jnp.float32),
        ],
        compiler_params=pltpu.CompilerParams(vmem_limit_bytes=24 * MIB),
        cost_estimate=pl.CostEstimate(flops=3_000_000_000, bytes_accessed=4_000_000, transcendentals=8_000_000),
        name="far_part",
    )(keep, got, before, after, cross, e, d, qt, gt, u, stat)


def unpack_kernel(rows, got_ref, q_ref, k_ref, v_ref):
    width = GROUP * HEAD
    for n in range(got_ref.shape[0]):
        for h in range(GROUP):
            q_ref[:, n * width + h * HEAD : n * width + (h + 1) * HEAD] = got_ref[n, h * rows : (h + 1) * rows, :]
        k_ref[:, n * HEAD : (n + 1) * HEAD] = got_ref[n, GROUP * rows : (GROUP + 1) * rows, :]
        v_ref[:, n * HEAD : (n + 1) * HEAD] = got_ref[n, (GROUP + 1) * rows :, :]


def unpack(got, rows):
    heads = got.shape[0]
    owners = 4
    return pl.pallas_call(
        functools.partial(unpack_kernel, rows),
        grid=(heads // owners,),
        in_specs=[pl.BlockSpec((owners,) + got.shape[1:], lambda n: (n, 0, 0))],
        out_specs=[
            pl.BlockSpec((rows, owners * GROUP * HEAD), lambda n: (0, n)),
            pl.BlockSpec((rows, owners * HEAD), lambda n: (0, n)),
            pl.BlockSpec((rows, owners * HEAD), lambda n: (0, n)),
        ],
        out_shape=[
            jax.ShapeDtypeStruct((rows, heads * GROUP * HEAD), jnp.bfloat16),
            jax.ShapeDtypeStruct((rows, heads * HEAD), jnp.bfloat16),
            jax.ShapeDtypeStruct((rows, heads * HEAD), jnp.bfloat16),
        ],
        name="unpack",
    )(got)


def local(queries, keys, values, output_gradient, outputs, block_order, doc_start):
    heads = lax.axis_size("head")
    seq_size = lax.axis_size("seq")
    rows = queries.shape[0]
    place = lax.axis_index("seq").astype(jnp.int32)
    keep = plan(place.reshape(1), block_order, doc_start, seq_size)
    got = swap_heads(pack(queries, keys, values, output_gradient, outputs, heads))
    kv = got[:, 2 * GROUP * rows + DELTA_ROWS :, :]
    kv, keep = lax.optimization_barrier((kv, keep))
    pair = swap_pair(kv)
    before, after, cross = send(kv, REACH), send(kv, -REACH), swap_cross(kv)
    state = near_part(keep, near(got), near(pair), rows)
    before, after, cross, *state = lax.optimization_barrier((before, after, cross, *state))
    *sums, out, own = far_part(
        keep, near(got), near(before), near(after), near(cross), [near(x) for x in state], rows
    )
    to_before, to_after, to_cross, to_pair = sums
    back = (send(to_before, -REACH), send(to_after, REACH), swap_cross(to_cross), swap_pair(to_pair))
    total = own
    for part in back:
        total = total + part.astype(jnp.float32)
    out = lax.dynamic_update_slice(out, total.astype(jnp.bfloat16), (0, GROUP * rows, 0))
    return tuple(unpack(swap_heads(out), rows))


def solution(mesh):
    rows = P(("seq", "head"), None)
    return jax.shard_map(
        local,
        mesh=mesh,
        in_specs=(rows, rows, rows, rows, rows, P(), P()),
        out_specs=(rows, rows, rows),
        check_vma=False,
    )
```

```python
import functools
import math

import jax
import jax.numpy as jnp
from jax import lax
from jax.experimental import pallas as pl
from jax.experimental.pallas import tpu as pltpu
from jax.sharding import PartitionSpec as P

QUERY_HEADS = 32
KEY_VALUE_HEADS = 8
GROUP = QUERY_HEADS // KEY_VALUE_HEADS
HEAD = 128
REACH = 2
BLK = 256
SCALE = 1.0 / math.sqrt(HEAD)
SCALE2 = SCALE * math.log2(math.e)
MASKED = -1e30
DELTA_ROWS = 16
MIB = 1024 * 1024
NEAR = 4
BLOCKS = 10


def send(value, steps):
    count = lax.axis_size("seq")
    return lax.ppermute(value, "seq", [(i, (i + steps) % count) for i in range(count)])


def swap_pair(value):
    count = lax.axis_size("seq")
    return lax.ppermute(value, "seq", [(i, i ^ 1) for i in range(count)])


def swap_cross(value):
    count = lax.axis_size("seq")
    return lax.ppermute(value, "seq", [(i, (i + (1 if i % 2 else count - 1)) % count) for i in range(count)])


def swap_heads(value):
    return lax.all_to_all(value, "head", split_axis=0, concat_axis=0, tiled=True)


def near_array(shape, dtype):
    return pltpu.VMEM(shape, dtype)


def in_hbm(value):
    return pltpu.with_memory_space_constraint(value, pltpu.HBM)


def near(value):
    return pltpu.with_memory_space_constraint(value, pltpu.VMEM)


SMEM = pl.BlockSpec(memory_space=pltpu.SMEM)
VMEM = pl.BlockSpec(memory_space=pltpu.VMEM)
HBM = pl.BlockSpec(memory_space=pltpu.HBM)


def pack_kernel(parts, q_in, g_in, o_in, k_in, v_in, out, out_ref, q_ref, g_ref, o_ref, k_ref, v_ref, sems):
    rows = q_ref.shape[0]
    owners = out_ref.shape[0]
    width = GROUP * HEAD
    base = 2 * GROUP * rows
    span = owners * width // parts
    wide = []
    for n in range(parts):
        for m, (a, b) in enumerate(((g_in, g_ref), (o_in, o_ref), (q_in, q_ref))):
            cols = pl.ds(n * span, span)
            wide.append(pltpu.make_async_copy(a.at[:, cols], b.at[:, cols], sems.at[3 * n + m]))
    narrow = [
        pltpu.make_async_copy(k_in, k_ref, sems.at[3 * parts]),
        pltpu.make_async_copy(v_in, v_ref, sems.at[3 * parts + 1]),
    ]
    for copy in wide[:3] + narrow + wide[3:]:
        copy.start()
    stores = []
    for n in range(owners):
        if n % (owners // parts) == 0:
            first = 3 * (n // (owners // parts))
            for copy in wide[first : first + 3]:
                copy.wait()
        products = []
        for h in range(GROUP):
            cols = slice(n * width + h * HEAD, n * width + (h + 1) * HEAD)
            grad = g_ref[:, cols]
            out_ref[n, h * rows : (h + 1) * rows, :] = q_ref[:, cols]
            out_ref[n, (GROUP + h) * rows : (GROUP + h + 1) * rows, :] = grad
            products.append(grad.astype(jnp.float32) * o_ref[:, cols].astype(jnp.float32))
        products = jnp.concatenate(products, axis=0)
        lead = products.astype(jnp.bfloat16)
        rest = (products - lead.astype(jnp.float32)).astype(jnp.bfloat16)
        ones = jnp.ones((8, HEAD), jnp.bfloat16)
        across = (((1,), (1,)), ((), ()))
        sums = lax.dot_general(ones, lead, across, preferred_element_type=jnp.float32)
        sums += lax.dot_general(ones, rest, across, preferred_element_type=jnp.float32)
        delta = jnp.concatenate([sums[0:1, :HEAD], sums[0:1, HEAD:]], axis=0)
        high = delta.astype(jnp.bfloat16).astype(jnp.float32)
        spare = jnp.zeros((DELTA_ROWS - GROUP, HEAD), jnp.float32)
        tile = jnp.concatenate([high, delta - high, spare], axis=0)
        out_ref[n, base : base + DELTA_ROWS, :] = tile.astype(jnp.bfloat16)
        if n == 0:
            for copy in narrow:
                copy.wait()
        at = base + DELTA_ROWS
        out_ref[n, at : at + rows, :] = k_ref[:, n * HEAD : (n + 1) * HEAD]
        out_ref[n, at + rows :, :] = v_ref[:, n * HEAD : (n + 1) * HEAD]
        if (n + 1) % (owners // parts) == 0:
            here = pl.ds(n + 1 - owners // parts, owners // parts)
            stores.append(pltpu.make_async_copy(out_ref.at[here], out.at[here], sems.at[3 * parts + 2 + len(stores)]))
            stores[-1].start()
    for copy in stores:
        copy.wait()


def pack(queries, keys, values, grads, outputs, heads):
    rows = queries.shape[0]
    parts = 2
    args = (queries, grads, outputs, keys, values)
    packed = (heads, (2 * GROUP + 2) * rows + DELTA_ROWS, HEAD)
    return pl.pallas_call(
        functools.partial(pack_kernel, parts),
        in_specs=[HBM] * 5,
        out_specs=HBM,
        out_shape=jax.ShapeDtypeStruct(packed, jnp.bfloat16),
        scratch_shapes=[pltpu.VMEM(packed, jnp.bfloat16)]
        + [pltpu.VMEM(x.shape, x.dtype) for x in args]
        + [pltpu.SemaphoreType.DMA((4 * parts + 2,))],
        compiler_params=pltpu.CompilerParams(vmem_limit_bytes=24 * MIB),
        name="pack",
    )(*[in_hbm(x) for x in args])


def plan_kernel(seq_size, mine_ref, order_ref, start_ref, keep_ref, docs_ref):
    def count(b, running):
        running = running + jnp.where(b > 0, start_ref[b], 0)
        docs_ref[b] = running
        return running

    lax.fori_loop(0, order_ref.shape[0], count, jnp.int32(0))
    mine = mine_ref[0]
    odd = lax.rem(mine, 2)
    steps = (0, 1 - 2 * odd, -REACH, REACH, 2 * odd - 1)
    blocks = []
    for step in steps:
        slab = lax.rem(mine + step + seq_size, seq_size)
        blocks += [order_ref[2 * slab], order_ref[2 * slab + 1]]
    docs = [docs_ref[b] for b in blocks]
    for i in range(2):
        for j in range(BLOCKS):
            kept = (blocks[j] <= blocks[i]) & (docs[j] == docs[i])
            keep_ref[i * BLOCKS + j] = kept.astype(jnp.int32)


def plan(mine, block_order, doc_start, seq_size):
    return pl.pallas_call(
        functools.partial(plan_kernel, seq_size),
        in_specs=[SMEM] * 3,
        out_specs=SMEM,
        out_shape=jax.ShapeDtypeStruct((2 * BLOCKS,), jnp.int32),
        scratch_shapes=[pltpu.SMEM((block_order.shape[0],), jnp.int32)],
        name="plan",
    )(mine, block_order, doc_start)


def block_of(ref, j, first, rows):
    per_block = BLK // rows
    tiles = ref[pl.ds(j * per_block, per_block), first : first + rows, :]
    return tiles.reshape(BLK, HEAD)


def near_kernel(
    rows, keep_ref, got_ref, pair_ref, e_own, d_own, e_pair, d_pair, qt_ref, gt_ref, u_ref, stat_ref, kv, scores
):
    per_block = BLK // rows
    chunk = GROUP * rows
    sources = 2 * per_block
    kv_at = 2 * chunk + DELTA_ROWS
    kv[:sources] = got_ref[:, kv_at:, :]
    kv[sources:] = pair_ref[...]

    def score(i, j, diagonal):
        keys = block_of(kv, j, 0, rows)
        for c in range(per_block):
            lanes = slice(c * chunk, (c + 1) * chunk)
            s = jnp.dot(keys, qt_ref[i, :, lanes], preferred_element_type=jnp.float32)
            if diagonal:
                key_at = lax.broadcasted_iota(jnp.int32, (BLK, chunk), 0)
                query_at = c * rows + lax.broadcasted_iota(jnp.int32, (BLK, chunk), 1) % rows
                s = jnp.where(key_at <= query_at, s, MASKED)
            scores[j, :, lanes] = s
            top = jnp.max(s, axis=0, keepdims=True)
            stat_ref[i, 0:1, lanes] = top if diagonal else jnp.maximum(top, stat_ref[i, 0:1, lanes])

    def weigh(i, j, first, own):
        keys_t = block_of(kv, j, 0, rows).T
        values = block_of(kv, j, rows, rows)
        parts = []
        for c in range(per_block):
            lanes = slice(c * chunk, (c + 1) * chunk)
            e = jnp.exp2((scores[j, :, lanes] - stat_ref[i, 0:1, lanes]) * SCALE2)
            total = jnp.sum(e, axis=0, keepdims=True)
            stat_ref[i, 1:2, lanes] = total if first else stat_ref[i, 1:2, lanes] + total
            dprobs = jnp.dot(values, gt_ref[i, :, lanes], preferred_element_type=jnp.float32)
            d = (e * (dprobs - stat_ref[i, 2:3, lanes])).astype(jnp.bfloat16)
            e_ref, d_ref, at = (e_own, d_own, 2 * i + j) if own else (e_pair, d_pair, 2 * i + j - 2)
            e_ref[at, :, lanes] = e.astype(jnp.bfloat16)
            d_ref[at, :, lanes] = d
            parts.append(d)
        u = jnp.dot(keys_t, jnp.concatenate(parts, axis=1), preferred_element_type=jnp.float32)
        u_ref[i] = u if first else u_ref[i] + u

    for i in range(2):
        for c in range(per_block):
            source = i * per_block + c
            lanes = slice(c * chunk, (c + 1) * chunk)
            qt_ref[i, :, lanes] = got_ref[source, :chunk, :].T
            gt_ref[i, :, lanes] = got_ref[source, chunk : 2 * chunk, :].T
            tile = got_ref[source, 2 * chunk : kv_at, :].astype(jnp.float32)
            delta = tile[0:2, :] + tile[2:4, :]
            stat_ref[i, 2:3, c * chunk : c * chunk + HEAD] = delta[0:1, :]
            stat_ref[i, 2:3, c * chunk + HEAD : (c + 1) * chunk] = delta[1:2, :]
        score(i, i, True)

        def visit_scores(j, _):
            @pl.when((keep_ref[i * BLOCKS + j] == 1) & (j != i))
            def _():
                score(i, j, False)

            return 0

        lax.fori_loop(0, NEAR, visit_scores, 0)
        weigh(i, i, True, True)

        @pl.when(keep_ref[i * BLOCKS + 1 - i] == 1)
        def _():
            weigh(i, 1 - i, False, True)

        def visit_weights(j, _):
            @pl.when(keep_ref[i * BLOCKS + j] == 1)
            def _():
                weigh(i, j, False, False)

            return 0

        lax.fori_loop(2, NEAR, visit_weights, 0)


def near_part(keep, got, pair, rows):
    lanes = BLK * GROUP
    return pl.pallas_call(
        functools.partial(near_kernel, rows),
        in_specs=[SMEM, VMEM, VMEM],
        out_specs=[VMEM] * 8,
        out_shape=[
            *[near_array((NEAR, BLK, lanes), jnp.bfloat16)] * 4,
            near_array((2, HEAD, lanes), jnp.bfloat16),
            near_array((2, HEAD, lanes), jnp.bfloat16),
            near_array((2, HEAD, lanes), jnp.float32),
            near_array((2, 8, lanes), jnp.float32),
        ],
        scratch_shapes=[
            pltpu.VMEM((2 * pair.shape[0],) + pair.shape[1:], jnp.bfloat16),
            pltpu.VMEM((NEAR, BLK, lanes), jnp.float32),
        ],
        compiler_params=pltpu.CompilerParams(vmem_limit_bytes=24 * MIB),
        cost_estimate=pl.CostEstimate(flops=3_000_000_000, bytes_accessed=4_000_000, transcendentals=8_000_000),
        name="near_part",
    )(keep, got, pair)


def far_kernel(
    rows, keep_ref, got_ref, before_ref, after_ref, cross_ref, e_ref, d_ref, qt_ref, gt_ref, u_ref,
    stat_ref, to_before, to_after, to_cross, to_pair, out_ref, alpha_ref, kv, scores, acc, stats, dqt_ref,
):
    per_block = BLK // rows
    chunk = GROUP * rows
    sources = 2 * per_block
    far_blocks = BLOCKS - NEAR
    kv[:sources] = before_ref[...]
    kv[sources : 2 * sources] = after_ref[...]

    kv[2 * sources :] = cross_ref[...]
    acc[...] = jnp.zeros_like(acc)

    def score(i, j):
        keys = block_of(kv, j, 0, rows)
        for c in range(per_block):
            lanes = slice(c * chunk, (c + 1) * chunk)
            s = jnp.dot(keys, qt_ref[i, :, lanes], preferred_element_type=jnp.float32)
            scores[j, :, lanes] = s
            before = stats[0:1, lanes]
            top = jnp.maximum(jnp.max(s, axis=0, keepdims=True), before)
            stats[0:1, lanes] = top
            stats[1:2, lanes] = stats[1:2, lanes] * jnp.exp2((before - top) * SCALE2) + jnp.sum(
                jnp.exp2((s - top) * SCALE2), axis=0, keepdims=True
            )

    def queries_of(i, first):
        tiles = got_ref[i * per_block : (i + 1) * per_block, first : first + chunk, :]
        return tiles.reshape(per_block * chunk, HEAD)

    def add(j, k, v):
        here = pl.ds(j * per_block, per_block)
        acc[here, :rows, :] += k.reshape(per_block, rows, HEAD)
        acc[here, rows:, :] += v.reshape(per_block, rows, HEAD)

    def gradients(i, j):
        keys_t = block_of(kv, j, 0, rows).T
        values = block_of(kv, j, rows, rows)
        all_p, all_d = [], []
        for c in range(per_block):
            lanes = slice(c * chunk, (c + 1) * chunk)
            probs = jnp.exp2(scores[j, :, lanes] * SCALE2 - stats[2:3, lanes])
            dprobs = jnp.dot(values, gt_ref[i, :, lanes], preferred_element_type=jnp.float32)
            all_d.append((probs * (dprobs - stat_ref[i, 2:3, lanes])).astype(jnp.bfloat16))
            all_p.append(probs.astype(jnp.bfloat16))
        probs = jnp.concatenate(all_p, axis=1)
        dscores = jnp.concatenate(all_d, axis=1)
        v = jnp.dot(probs, queries_of(i, chunk), preferred_element_type=jnp.float32)
        k = jnp.dot(dscores, queries_of(i, 0), preferred_element_type=jnp.float32)
        dqt_ref[i] += jnp.dot(keys_t, dscores, preferred_element_type=jnp.float32)
        add(j, k, v)

    def pair_gradients(i, j):
        p = (e_ref[2 * i + j].astype(jnp.float32) * alpha_ref[i, 0:1, :]).astype(jnp.bfloat16)
        d = (d_ref[2 * i + j].astype(jnp.float32) * alpha_ref[i, 0:1, :]).astype(jnp.bfloat16)
        v = jnp.dot(p, queries_of(i, chunk), preferred_element_type=jnp.float32)
        k = jnp.dot(d, queries_of(i, 0), preferred_element_type=jnp.float32)
        add(far_blocks + j, k, v)

    for i in range(2):
        stats[0:2, :] = stat_ref[i, 0:2, :]

        def visit_scores(j, _):
            @pl.when(keep_ref[i * BLOCKS + NEAR + j] == 1)
            def _():
                score(i, j)

            return 0

        lax.fori_loop(0, far_blocks, visit_scores, 0)
        lse = stats[0:1, :] * SCALE2 + jnp.log2(stats[1:2, :])
        stats[2:3, :] = lse
        alpha = jnp.exp2(stat_ref[i, 0:1, :] * SCALE2 - lse)
        alpha_ref[i, 0:1, :] = alpha
        dqt_ref[i] = u_ref[i] * alpha

        def visit_gradients(j, _):
            @pl.when(keep_ref[i * BLOCKS + NEAR + j] == 1)
            def _():
                gradients(i, j)

            return 0

        lax.fori_loop(0, far_blocks, visit_gradients, 0)

        def visit_pair(j, _):
            @pl.when(keep_ref[i * BLOCKS + 2 + j] == 1)
            def _():
                pair_gradients(i, j)

            return 0

        lax.fori_loop(0, 2, visit_pair, 0)
        for c in range(per_block):
            dq = (dqt_ref[i, :, c * chunk : (c + 1) * chunk] * SCALE).T
            out_ref[i * per_block + c, :chunk, :] = dq.astype(jnp.bfloat16)

    for n, ref in enumerate((to_before, to_after, to_cross, to_pair)):
        here = slice(n * sources, (n + 1) * sources)
        ref[:, :rows, :] = (acc[here, :rows, :] * SCALE).astype(jnp.bfloat16)
        ref[:, rows:, :] = acc[here, rows:, :].astype(jnp.bfloat16)


def far_part(keep, got, before, after, cross, state, rows):
    lanes = BLK * GROUP
    e, d, qt, gt, u, stat = state
    chunk = GROUP * rows
    sources, tall, _ = before.shape
    return pl.pallas_call(
        functools.partial(far_kernel, rows),
        in_specs=[SMEM] + [VMEM] * 10,
        out_specs=[VMEM] * 6,
        out_shape=[
            *[jax.ShapeDtypeStruct((sources, tall, HEAD), jnp.bfloat16)] * 4,
            jax.ShapeDtypeStruct((sources, chunk + tall, HEAD), jnp.bfloat16),
            jax.ShapeDtypeStruct((2, 8, lanes), jnp.float32),
        ],
        scratch_shapes=[
            pltpu.VMEM((3 * sources, tall, HEAD), jnp.bfloat16),
            pltpu.VMEM((BLOCKS - NEAR, BLK, lanes), jnp.float32),
            pltpu.VMEM((4 * sources, tall, HEAD), jnp.float32),
            pltpu.VMEM((8, lanes), jnp.float32),
            pltpu.VMEM((2, HEAD, lanes), jnp.float32),
        ],
        compiler_params=pltpu.CompilerParams(vmem_limit_bytes=24 * MIB),
        cost_estimate=pl.CostEstimate(flops=3_000_000_000, bytes_accessed=4_000_000, transcendentals=8_000_000),
        name="far_part",
    )(keep, got, before, after, cross, e, d, qt, gt, u, stat)


def own_kernel(rows, keep_ref, got_ref, e_in, d_in, alpha_ref, own_ref, e_ref, d_ref, sems):
    per_block = BLK // rows
    chunk = GROUP * rows

    def copies(n):
        return (
            pltpu.make_async_copy(e_in.at[n], e_ref.at[n], sems.at[n]),
            pltpu.make_async_copy(d_in.at[n], d_ref.at[n], sems.at[NEAR + n]),
        )

    def when_kept(visit):
        for i in range(2):
            for j in range(2):
                if i == j:
                    visit(i, j)
                else:
                    pl.when(keep_ref[i * BLOCKS + j] == 1)(functools.partial(visit, i, j))

    def load(i, j):
        for copy in copies(2 * i + j):
            copy.start()

    def add(i, j):
        for copy in copies(2 * i + j):
            copy.wait()
        p = (e_ref[2 * i + j].astype(jnp.float32) * alpha_ref[i, 0:1, :]).astype(jnp.bfloat16)
        d = (d_ref[2 * i + j].astype(jnp.float32) * alpha_ref[i, 0:1, :]).astype(jnp.bfloat16)
        tiles = got_ref[i * per_block : (i + 1) * per_block, : 2 * chunk, :]
        q = tiles[:, :chunk, :].reshape(per_block * chunk, HEAD)
        g = tiles[:, chunk:, :].reshape(per_block * chunk, HEAD)
        v = jnp.dot(p, g, preferred_element_type=jnp.float32)
        k = jnp.dot(d, q, preferred_element_type=jnp.float32) * SCALE
        here = slice(j * per_block, (j + 1) * per_block)
        own_ref[here, :rows, :] += k.reshape(per_block, rows, HEAD)
        own_ref[here, rows:, :] += v.reshape(per_block, rows, HEAD)

    when_kept(load)
    own_ref[...] = jnp.zeros_like(own_ref)
    when_kept(add)


def own_part(keep, got, e, d, alpha, rows):
    return pl.pallas_call(
        functools.partial(own_kernel, rows),
        in_specs=[SMEM, VMEM, HBM, HBM, VMEM],
        out_specs=VMEM,
        out_shape=jax.ShapeDtypeStruct((got.shape[0], 2 * rows, HEAD), jnp.float32),
        scratch_shapes=[
            pltpu.VMEM(e.shape, e.dtype),
            pltpu.VMEM(d.shape, d.dtype),
            pltpu.SemaphoreType.DMA((2 * NEAR,)),
        ],
        compiler_params=pltpu.CompilerParams(vmem_limit_bytes=16 * MIB),
        cost_estimate=pl.CostEstimate(flops=1_000_000_000, bytes_accessed=4_000_000, transcendentals=0),
        name="own_part",
    )(keep, got, in_hbm(e), in_hbm(d), alpha)


def unpack_kernel(rows, parts, got_ref, q_out, k_out, v_out, q_ref, k_ref, v_ref, sems):
    owners = got_ref.shape[0]
    width = GROUP * HEAD
    copies = []
    for n in range(owners):
        for h in range(GROUP):
            q_ref[:, n * width + h * HEAD : n * width + (h + 1) * HEAD] = got_ref[n, h * rows : (h + 1) * rows, :]
        k_ref[:, n * HEAD : (n + 1) * HEAD] = got_ref[n, GROUP * rows : (GROUP + 1) * rows, :]
        v_ref[:, n * HEAD : (n + 1) * HEAD] = got_ref[n, (GROUP + 1) * rows :, :]
        if (n + 1) % (owners // parts) == 0:
            span = owners * width // parts
            cols = pl.ds((n + 1) * width - span, span)
            copies.append(pltpu.make_async_copy(q_ref.at[:, cols], q_out.at[:, cols], sems.at[len(copies)]))
            copies[-1].start()
    copies.append(pltpu.make_async_copy(k_ref, k_out, sems.at[parts]))
    copies.append(pltpu.make_async_copy(v_ref, v_out, sems.at[parts + 1]))
    copies[-2].start()
    copies[-1].start()
    for copy in copies:
        copy.wait()


def unpack(got, rows):
    heads = got.shape[0]
    parts = 4
    shapes = [(rows, heads * GROUP * HEAD), (rows, heads * HEAD), (rows, heads * HEAD)]
    return pl.pallas_call(
        functools.partial(unpack_kernel, rows, parts),
        in_specs=[VMEM],
        out_specs=[HBM] * 3,
        out_shape=[jax.ShapeDtypeStruct(x, jnp.bfloat16) for x in shapes],
        scratch_shapes=[pltpu.VMEM(x, jnp.bfloat16) for x in shapes] + [pltpu.SemaphoreType.DMA((parts + 2,))],
        compiler_params=pltpu.CompilerParams(vmem_limit_bytes=16 * MIB),
        name="unpack",
    )(near(got))


def local(queries, keys, values, output_gradient, outputs, block_order, doc_start):
    heads = lax.axis_size("head")
    seq_size = lax.axis_size("seq")
    rows = queries.shape[0]
    place = lax.axis_index("seq").astype(jnp.int32)
    keep = plan(place.reshape(1), block_order, doc_start, seq_size)
    got = swap_heads(pack(queries, keys, values, output_gradient, outputs, heads))
    kv = got[:, 2 * GROUP * rows + DELTA_ROWS :, :]
    kv, keep = lax.optimization_barrier((kv, keep))
    cross, after, before = swap_cross(kv), send(kv, -REACH), send(kv, REACH)
    pair = swap_pair(kv)
    state = near_part(keep, near(got), near(pair), rows)
    e_own, d_own, *state = state
    cross, after, before, *state = lax.optimization_barrier((cross, after, before, *state))
    *sums, out, alpha = far_part(
        keep, near(got), near(before), near(after), near(cross), [near(x) for x in state], rows
    )
    to_before, to_after, to_cross, to_pair = sums
    back = (send(to_before, -REACH), send(to_after, REACH), swap_cross(to_cross), swap_pair(to_pair))
    total = own_part(keep, got, e_own, d_own, alpha, rows)
    for part in back:
        total = total + part.astype(jnp.float32)
    out = lax.dynamic_update_slice(out, total.astype(jnp.bfloat16), (0, GROUP * rows, 0))
    return tuple(unpack(swap_heads(out), rows))


def solution(mesh):
    rows = P(("seq", "head"), None)
    return jax.shard_map(
        local,
        mesh=mesh,
        in_specs=(rows, rows, rows, rows, rows, P(), P()),
        out_specs=(rows, rows, rows),
        check_vma=False,
    )
```

```python
import functools
import math

import jax
import jax.numpy as jnp
from jax import lax
from jax.experimental import pallas as pl
from jax.experimental.pallas import tpu as pltpu
from jax.sharding import PartitionSpec as P

QUERY_HEADS = 32
KEY_VALUE_HEADS = 8
GROUP = QUERY_HEADS // KEY_VALUE_HEADS
HEAD = 128
REACH = 2
BLK = 256
SCALE = 1.0 / math.sqrt(HEAD)
SCALE2 = SCALE * math.log2(math.e)
MASKED = -1e30
DELTA_ROWS = 16
MIB = 1024 * 1024
NEAR = 4
BLOCKS = 10


def send(value, steps):
    count = lax.axis_size("seq")
    return lax.ppermute(value, "seq", [(i, (i + steps) % count) for i in range(count)])


def swap_pair(value):
    count = lax.axis_size("seq")
    return lax.ppermute(value, "seq", [(i, i ^ 1) for i in range(count)])


def swap_cross(value):
    count = lax.axis_size("seq")
    return lax.ppermute(value, "seq", [(i, (i + (1 if i % 2 else count - 1)) % count) for i in range(count)])


def swap_heads(value):
    return lax.all_to_all(value, "head", split_axis=0, concat_axis=0, tiled=True)


def near_array(shape, dtype):
    return pltpu.VMEM(shape, dtype)


def in_hbm(value):
    return pltpu.with_memory_space_constraint(value, pltpu.HBM)


def near(value):
    return pltpu.with_memory_space_constraint(value, pltpu.VMEM)


SMEM = pl.BlockSpec(memory_space=pltpu.SMEM)
VMEM = pl.BlockSpec(memory_space=pltpu.VMEM)
HBM = pl.BlockSpec(memory_space=pltpu.HBM)


def pack_kernel(parts, q_in, g_in, o_in, k_in, v_in, out, out_ref, q_ref, g_ref, o_ref, k_ref, v_ref, sems):
    rows = q_ref.shape[0]
    owners = out_ref.shape[0]
    width = GROUP * HEAD
    base = 2 * GROUP * rows
    span = owners * width // parts
    wide = []
    for n in range(parts):
        for m, (a, b) in enumerate(((g_in, g_ref), (o_in, o_ref), (q_in, q_ref))):
            cols = pl.ds(n * span, span)
            wide.append(pltpu.make_async_copy(a.at[:, cols], b.at[:, cols], sems.at[3 * n + m]))
    narrow = [
        pltpu.make_async_copy(k_in, k_ref, sems.at[3 * parts]),
        pltpu.make_async_copy(v_in, v_ref, sems.at[3 * parts + 1]),
    ]
    for copy in wide[:3] + narrow + wide[3:]:
        copy.start()
    stores = []
    for n in range(owners):
        if n % (owners // parts) == 0:
            first = 3 * (n // (owners // parts))
            for copy in wide[first : first + 3]:
                copy.wait()
        products = []
        for h in range(GROUP):
            cols = slice(n * width + h * HEAD, n * width + (h + 1) * HEAD)
            grad = g_ref[:, cols]
            out_ref[n, h * rows : (h + 1) * rows, :] = q_ref[:, cols]
            out_ref[n, (GROUP + h) * rows : (GROUP + h + 1) * rows, :] = grad
            products.append(grad.astype(jnp.float32) * o_ref[:, cols].astype(jnp.float32))
        products = jnp.concatenate(products, axis=0)
        lead = products.astype(jnp.bfloat16)
        rest = (products - lead.astype(jnp.float32)).astype(jnp.bfloat16)
        ones = jnp.ones((8, HEAD), jnp.bfloat16)
        across = (((1,), (1,)), ((), ()))
        sums = lax.dot_general(ones, lead, across, preferred_element_type=jnp.float32)
        sums += lax.dot_general(ones, rest, across, preferred_element_type=jnp.float32)
        delta = jnp.concatenate([sums[0:1, :HEAD], sums[0:1, HEAD:]], axis=0)
        high = delta.astype(jnp.bfloat16).astype(jnp.float32)
        spare = jnp.zeros((DELTA_ROWS - GROUP, HEAD), jnp.float32)
        tile = jnp.concatenate([high, delta - high, spare], axis=0)
        out_ref[n, base : base + DELTA_ROWS, :] = tile.astype(jnp.bfloat16)
        if n == 0:
            for copy in narrow:
                copy.wait()
        at = base + DELTA_ROWS
        out_ref[n, at : at + rows, :] = k_ref[:, n * HEAD : (n + 1) * HEAD]
        out_ref[n, at + rows :, :] = v_ref[:, n * HEAD : (n + 1) * HEAD]
        if (n + 1) % (owners // parts) == 0:
            here = pl.ds(n + 1 - owners // parts, owners // parts)
            stores.append(pltpu.make_async_copy(out_ref.at[here], out.at[here], sems.at[3 * parts + 2 + len(stores)]))
            stores[-1].start()
    for copy in stores:
        copy.wait()


def pack(queries, keys, values, grads, outputs, heads):
    rows = queries.shape[0]
    parts = 2
    args = (queries, grads, outputs, keys, values)
    packed = (heads, (2 * GROUP + 2) * rows + DELTA_ROWS, HEAD)
    return pl.pallas_call(
        functools.partial(pack_kernel, parts),
        in_specs=[HBM] * 5,
        out_specs=HBM,
        out_shape=jax.ShapeDtypeStruct(packed, jnp.bfloat16),
        scratch_shapes=[pltpu.VMEM(packed, jnp.bfloat16)]
        + [pltpu.VMEM(x.shape, x.dtype) for x in args]
        + [pltpu.SemaphoreType.DMA((4 * parts + 2,))],
        compiler_params=pltpu.CompilerParams(vmem_limit_bytes=24 * MIB),
        name="pack",
    )(*[in_hbm(x) for x in args])


def plan_kernel(seq_size, mine_ref, order_ref, start_ref, keep_ref, docs_ref):
    def count(b, running):
        running = running + jnp.where(b > 0, start_ref[b], 0)
        docs_ref[b] = running
        return running

    lax.fori_loop(0, order_ref.shape[0], count, jnp.int32(0))
    mine = mine_ref[0]
    odd = lax.rem(mine, 2)
    steps = (0, 1 - 2 * odd, -REACH, REACH, 2 * odd - 1)
    blocks = []
    for step in steps:
        slab = lax.rem(mine + step + seq_size, seq_size)
        blocks += [order_ref[2 * slab], order_ref[2 * slab + 1]]
    docs = [docs_ref[b] for b in blocks]
    for i in range(2):
        for j in range(BLOCKS):
            kept = (blocks[j] <= blocks[i]) & (docs[j] == docs[i])
            keep_ref[i * BLOCKS + j] = kept.astype(jnp.int32)


def plan(mine, block_order, doc_start, seq_size):
    return pl.pallas_call(
        functools.partial(plan_kernel, seq_size),
        in_specs=[SMEM] * 3,
        out_specs=SMEM,
        out_shape=jax.ShapeDtypeStruct((2 * BLOCKS,), jnp.int32),
        scratch_shapes=[pltpu.SMEM((block_order.shape[0],), jnp.int32)],
        name="plan",
    )(mine, block_order, doc_start)


def block_of(ref, j, first, rows):
    per_block = BLK // rows
    tiles = ref[pl.ds(j * per_block, per_block), first : first + rows, :]
    return tiles.reshape(BLK, HEAD)


def near_kernel(
    rows, keep_ref, got_ref, pair_ref, e_own, d_own, e_pair, d_pair, qt_ref, gt_ref, u_ref, stat_ref, kv, scores
):
    per_block = BLK // rows
    chunk = GROUP * rows
    sources = 2 * per_block
    kv_at = 2 * chunk + DELTA_ROWS
    kv[:sources] = got_ref[:, kv_at:, :]
    kv[sources:] = pair_ref[...]

    def score(i, j, diagonal):
        keys = block_of(kv, j, 0, rows)
        for c in range(per_block):
            lanes = slice(c * chunk, (c + 1) * chunk)
            s = jnp.dot(keys, qt_ref[i, :, lanes], preferred_element_type=jnp.float32)
            if diagonal:
                key_at = lax.broadcasted_iota(jnp.int32, (BLK, chunk), 0)
                query_at = c * rows + lax.broadcasted_iota(jnp.int32, (BLK, chunk), 1) % rows
                s = jnp.where(key_at <= query_at, s, MASKED)
            scores[j, :, lanes] = s
            top = jnp.max(s, axis=0, keepdims=True)
            stat_ref[i, 0:1, lanes] = top if diagonal else jnp.maximum(top, stat_ref[i, 0:1, lanes])

    def weigh(i, j, first, own):
        keys_t = block_of(kv, j, 0, rows).T
        values = block_of(kv, j, rows, rows)
        parts = []
        for c in range(per_block):
            lanes = slice(c * chunk, (c + 1) * chunk)
            e = jnp.exp2((scores[j, :, lanes] - stat_ref[i, 0:1, lanes]) * SCALE2)
            total = jnp.sum(e, axis=0, keepdims=True)
            stat_ref[i, 1:2, lanes] = total if first else stat_ref[i, 1:2, lanes] + total
            dprobs = jnp.dot(values, gt_ref[i, :, lanes], preferred_element_type=jnp.float32)
            d = (e * (dprobs - stat_ref[i, 2:3, lanes])).astype(jnp.bfloat16)
            e_ref, d_ref, at = (e_own, d_own, 2 * i + j) if own else (e_pair, d_pair, 2 * i + j - 2)
            e_ref[at, :, lanes] = e.astype(jnp.bfloat16)
            d_ref[at, :, lanes] = d
            parts.append(d)
        u = jnp.dot(keys_t, jnp.concatenate(parts, axis=1), preferred_element_type=jnp.float32)
        u_ref[i] = u if first else u_ref[i] + u

    for i in range(2):
        for c in range(per_block):
            source = i * per_block + c
            lanes = slice(c * chunk, (c + 1) * chunk)
            qt_ref[i, :, lanes] = got_ref[source, :chunk, :].T
            gt_ref[i, :, lanes] = got_ref[source, chunk : 2 * chunk, :].T
            tile = got_ref[source, 2 * chunk : kv_at, :].astype(jnp.float32)
            delta = tile[0:2, :] + tile[2:4, :]
            stat_ref[i, 2:3, c * chunk : c * chunk + HEAD] = delta[0:1, :]
            stat_ref[i, 2:3, c * chunk + HEAD : (c + 1) * chunk] = delta[1:2, :]
        score(i, i, True)

        def visit_scores(j, _):
            @pl.when((keep_ref[i * BLOCKS + j] == 1) & (j != i))
            def _():
                score(i, j, False)

            return 0

        lax.fori_loop(0, NEAR, visit_scores, 0)
        weigh(i, i, True, True)

        @pl.when(keep_ref[i * BLOCKS + 1 - i] == 1)
        def _():
            weigh(i, 1 - i, False, True)

        def visit_weights(j, _):
            @pl.when(keep_ref[i * BLOCKS + j] == 1)
            def _():
                weigh(i, j, False, False)

            return 0

        lax.fori_loop(2, NEAR, visit_weights, 0)


def near_part(keep, got, pair, rows):
    lanes = BLK * GROUP
    return pl.pallas_call(
        functools.partial(near_kernel, rows),
        in_specs=[SMEM, VMEM, VMEM],
        out_specs=[VMEM] * 8,
        out_shape=[
            *[jax.ShapeDtypeStruct((NEAR, BLK, lanes), jnp.bfloat16)] * 4,
            jax.ShapeDtypeStruct((2, HEAD, lanes), jnp.bfloat16),
            jax.ShapeDtypeStruct((2, HEAD, lanes), jnp.bfloat16),
            jax.ShapeDtypeStruct((2, HEAD, lanes), jnp.float32),
            jax.ShapeDtypeStruct((2, 8, lanes), jnp.float32),
        ],
        scratch_shapes=[
            pltpu.VMEM((2 * pair.shape[0],) + pair.shape[1:], jnp.bfloat16),
            pltpu.VMEM((NEAR, BLK, lanes), jnp.float32),
        ],
        compiler_params=pltpu.CompilerParams(vmem_limit_bytes=24 * MIB),
        cost_estimate=pl.CostEstimate(flops=3_000_000_000, bytes_accessed=4_000_000, transcendentals=8_000_000),
        name="near_part",
    )(keep, got, pair)


def far_kernel(
    rows, keep_ref, got_ref, before_ref, after_ref, cross_ref, e_ref, d_ref, qt_ref, gt_ref, u_ref,
    stat_ref, to_before, to_after, to_cross, to_pair, dqt_ref, alpha_ref, kv, scores, acc, stats,
):
    per_block = BLK // rows
    chunk = GROUP * rows
    sources = 2 * per_block
    far_blocks = BLOCKS - NEAR
    kv[:sources] = before_ref[...]
    kv[sources : 2 * sources] = after_ref[...]

    kv[2 * sources :] = cross_ref[...]
    acc[...] = jnp.zeros_like(acc)

    def score(i, j):
        keys = block_of(kv, j, 0, rows)
        for c in range(per_block):
            lanes = slice(c * chunk, (c + 1) * chunk)
            s = jnp.dot(keys, qt_ref[i, :, lanes], preferred_element_type=jnp.float32)
            scores[j, :, lanes] = s
            before = stats[0:1, lanes]
            top = jnp.maximum(jnp.max(s, axis=0, keepdims=True), before)
            stats[0:1, lanes] = top
            stats[1:2, lanes] = stats[1:2, lanes] * jnp.exp2((before - top) * SCALE2) + jnp.sum(
                jnp.exp2((s - top) * SCALE2), axis=0, keepdims=True
            )

    def queries_of(i, first):
        tiles = got_ref[i * per_block : (i + 1) * per_block, first : first + chunk, :]
        return tiles.reshape(per_block * chunk, HEAD)

    def add(j, k, v):
        here = pl.ds(j * per_block, per_block)
        acc[here, :rows, :] += k.reshape(per_block, rows, HEAD)
        acc[here, rows:, :] += v.reshape(per_block, rows, HEAD)

    def gradients(i, j):
        keys_t = block_of(kv, j, 0, rows).T
        values = block_of(kv, j, rows, rows)
        all_p, all_d = [], []
        for c in range(per_block):
            lanes = slice(c * chunk, (c + 1) * chunk)
            probs = jnp.exp2(scores[j, :, lanes] * SCALE2 - stats[2:3, lanes])
            dprobs = jnp.dot(values, gt_ref[i, :, lanes], preferred_element_type=jnp.float32)
            all_d.append((probs * (dprobs - stat_ref[i, 2:3, lanes])).astype(jnp.bfloat16))
            all_p.append(probs.astype(jnp.bfloat16))
        probs = jnp.concatenate(all_p, axis=1)
        dscores = jnp.concatenate(all_d, axis=1)
        v = jnp.dot(probs, queries_of(i, chunk), preferred_element_type=jnp.float32)
        k = jnp.dot(dscores, queries_of(i, 0), preferred_element_type=jnp.float32)
        dqt_ref[i] += jnp.dot(keys_t, dscores, preferred_element_type=jnp.float32)
        add(j, k, v)

    def pair_gradients(i, j):
        p = (e_ref[2 * i + j].astype(jnp.float32) * alpha_ref[i, 0:1, :]).astype(jnp.bfloat16)
        d = (d_ref[2 * i + j].astype(jnp.float32) * alpha_ref[i, 0:1, :]).astype(jnp.bfloat16)
        v = jnp.dot(p, queries_of(i, chunk), preferred_element_type=jnp.float32)
        k = jnp.dot(d, queries_of(i, 0), preferred_element_type=jnp.float32)
        add(far_blocks + j, k, v)

    for i in range(2):
        stats[0:2, :] = stat_ref[i, 0:2, :]

        def visit_scores(j, _):
            @pl.when(keep_ref[i * BLOCKS + NEAR + j] == 1)
            def _():
                score(i, j)

            return 0

        lax.fori_loop(0, far_blocks, visit_scores, 0)
        lse = stats[0:1, :] * SCALE2 + jnp.log2(stats[1:2, :])
        stats[2:3, :] = lse
        alpha = jnp.exp2(stat_ref[i, 0:1, :] * SCALE2 - lse)
        alpha_ref[i, 0:1, :] = alpha
        dqt_ref[i] = u_ref[i] * alpha

        def visit_gradients(j, _):
            @pl.when(keep_ref[i * BLOCKS + NEAR + j] == 1)
            def _():
                gradients(i, j)

            return 0

        lax.fori_loop(0, far_blocks, visit_gradients, 0)

        def visit_pair(j, _):
            @pl.when(keep_ref[i * BLOCKS + 2 + j] == 1)
            def _():
                pair_gradients(i, j)

            return 0

        lax.fori_loop(0, 2, visit_pair, 0)

    for n, ref in enumerate((to_before, to_after, to_cross, to_pair)):
        here = slice(n * sources, (n + 1) * sources)
        ref[:, :rows, :] = (acc[here, :rows, :] * SCALE).astype(jnp.bfloat16)
        ref[:, rows:, :] = acc[here, rows:, :].astype(jnp.bfloat16)


def far_part(keep, got, before, after, cross, state, rows):
    lanes = BLK * GROUP
    e, d, qt, gt, u, stat = state
    sources, tall, _ = before.shape
    return pl.pallas_call(
        functools.partial(far_kernel, rows),
        in_specs=[SMEM] + [VMEM] * 10,
        out_specs=[VMEM] * 6,
        out_shape=[
            *[jax.ShapeDtypeStruct((sources, tall, HEAD), jnp.bfloat16)] * 4,
            jax.ShapeDtypeStruct((2, HEAD, lanes), jnp.float32),
            jax.ShapeDtypeStruct((2, 8, lanes), jnp.float32),
        ],
        scratch_shapes=[
            pltpu.VMEM((3 * sources, tall, HEAD), jnp.bfloat16),
            pltpu.VMEM((BLOCKS - NEAR, BLK, lanes), jnp.float32),
            pltpu.VMEM((4 * sources, tall, HEAD), jnp.float32),
            pltpu.VMEM((8, lanes), jnp.float32),
        ],
        compiler_params=pltpu.CompilerParams(vmem_limit_bytes=24 * MIB),
        cost_estimate=pl.CostEstimate(flops=3_000_000_000, bytes_accessed=4_000_000, transcendentals=8_000_000),
        name="far_part",
    )(keep, got, before, after, cross, e, d, qt, gt, u, stat)


def own_kernel(rows, keep_ref, got_ref, e_ref, d_ref, dqt_ref, alpha_ref, own_ref, out_ref):
    per_block = BLK // rows
    chunk = GROUP * rows

    def add(i, j):
        p = (e_ref[2 * i + j].astype(jnp.float32) * alpha_ref[i, 0:1, :]).astype(jnp.bfloat16)
        d = (d_ref[2 * i + j].astype(jnp.float32) * alpha_ref[i, 0:1, :]).astype(jnp.bfloat16)
        tiles = got_ref[i * per_block : (i + 1) * per_block, : 2 * chunk, :]
        q = tiles[:, :chunk, :].reshape(per_block * chunk, HEAD)
        g = tiles[:, chunk:, :].reshape(per_block * chunk, HEAD)
        v = jnp.dot(p, g, preferred_element_type=jnp.float32)
        k = jnp.dot(d, q, preferred_element_type=jnp.float32) * SCALE
        here = slice(j * per_block, (j + 1) * per_block)
        own_ref[here, :rows, :] += k.reshape(per_block, rows, HEAD)
        own_ref[here, rows:, :] += v.reshape(per_block, rows, HEAD)

    own_ref[...] = jnp.zeros_like(own_ref)
    for i in range(2):
        add(i, i)
        pl.when(keep_ref[i * BLOCKS + 1 - i] == 1)(functools.partial(add, i, 1 - i))
        for c in range(per_block):
            dq = (dqt_ref[i, :, c * chunk : (c + 1) * chunk] * SCALE).T
            out_ref[i * per_block + c, :chunk, :] = dq.astype(jnp.bfloat16)


def own_part(keep, got, e, d, dqt, alpha, rows):
    return pl.pallas_call(
        functools.partial(own_kernel, rows),
        in_specs=[SMEM] + [VMEM] * 5,
        out_specs=[VMEM] * 2,
        out_shape=[
            jax.ShapeDtypeStruct((got.shape[0], 2 * rows, HEAD), jnp.float32),
            jax.ShapeDtypeStruct((got.shape[0], (GROUP + 2) * rows, HEAD), jnp.bfloat16),
        ],
        compiler_params=pltpu.CompilerParams(vmem_limit_bytes=16 * MIB),
        cost_estimate=pl.CostEstimate(flops=1_000_000_000, bytes_accessed=4_000_000, transcendentals=0),
        name="own_part",
    )(keep, got, e, d, dqt, alpha)


def unpack_kernel(rows, parts, got_ref, q_out, k_out, v_out, q_ref, k_ref, v_ref, sems):
    owners = got_ref.shape[0]
    width = GROUP * HEAD
    copies = []
    for n in range(owners):
        for h in range(GROUP):
            q_ref[:, n * width + h * HEAD : n * width + (h + 1) * HEAD] = got_ref[n, h * rows : (h + 1) * rows, :]
        k_ref[:, n * HEAD : (n + 1) * HEAD] = got_ref[n, GROUP * rows : (GROUP + 1) * rows, :]
        v_ref[:, n * HEAD : (n + 1) * HEAD] = got_ref[n, (GROUP + 1) * rows :, :]
        if (n + 1) % (owners // parts) == 0:
            span = owners * width // parts
            cols = pl.ds((n + 1) * width - span, span)
            copies.append(pltpu.make_async_copy(q_ref.at[:, cols], q_out.at[:, cols], sems.at[len(copies)]))
            copies[-1].start()
    copies.append(pltpu.make_async_copy(k_ref, k_out, sems.at[parts]))
    copies.append(pltpu.make_async_copy(v_ref, v_out, sems.at[parts + 1]))
    copies[-2].start()
    copies[-1].start()
    for copy in copies:
        copy.wait()


def unpack(got, rows):
    heads = got.shape[0]
    parts = 4
    shapes = [(rows, heads * GROUP * HEAD), (rows, heads * HEAD), (rows, heads * HEAD)]
    return pl.pallas_call(
        functools.partial(unpack_kernel, rows, parts),
        in_specs=[VMEM],
        out_specs=[HBM] * 3,
        out_shape=[jax.ShapeDtypeStruct(x, jnp.bfloat16) for x in shapes],
        scratch_shapes=[pltpu.VMEM(x, jnp.bfloat16) for x in shapes] + [pltpu.SemaphoreType.DMA((parts + 2,))],
        compiler_params=pltpu.CompilerParams(vmem_limit_bytes=16 * MIB),
        name="unpack",
    )(got)


def local(queries, keys, values, output_gradient, outputs, block_order, doc_start):
    heads = lax.axis_size("head")
    seq_size = lax.axis_size("seq")
    rows = queries.shape[0]
    place = lax.axis_index("seq").astype(jnp.int32)
    keep = plan(place.reshape(1), block_order, doc_start, seq_size)
    got = swap_heads(pack(queries, keys, values, output_gradient, outputs, heads))
    kv = got[:, 2 * GROUP * rows + DELTA_ROWS :, :]
    kv, keep = lax.optimization_barrier((kv, keep))
    after, before = send(kv, -REACH), send(kv, REACH)
    pair = swap_pair(kv)
    state = near_part(keep, got, pair, rows)
    e_own, d_own, *state = state
    after, before, *state = lax.optimization_barrier((after, before, *state))
    cross = swap_pair(jnp.where(lax.rem(place, 2) == 1, before, after))
    *sums, dqt, alpha = far_part(
        keep, got, before, after, cross, state, rows
    )
    to_before, to_after, to_cross, to_pair = sums
    back = (send(to_before, -REACH), send(to_after, REACH), swap_cross(to_cross), swap_pair(to_pair))
    total, out = own_part(keep, got, e_own, d_own, dqt, alpha, rows)
    for part in back:
        total = total + part.astype(jnp.float32)
    out = lax.dynamic_update_slice(out, total.astype(jnp.bfloat16), (0, GROUP * rows, 0))
    return tuple(unpack(swap_heads(out), rows))


def solution(mesh):
    rows = P(("seq", "head"), None)
    return jax.shard_map(
        local,
        mesh=mesh,
        in_specs=(rows, rows, rows, rows, rows, P(), P()),
        out_specs=(rows, rows, rows),
        check_vma=False,
    )
```

```python
import functools
import math

import jax
import jax.numpy as jnp
from jax import lax
from jax.experimental import pallas as pl
from jax.experimental.pallas import tpu as pltpu
from jax.sharding import PartitionSpec as P

QUERY_HEADS = 32
KEY_VALUE_HEADS = 8
GROUP = QUERY_HEADS // KEY_VALUE_HEADS
HEAD = 128
REACH = 2
BLK = 256
SCALE = 1.0 / math.sqrt(HEAD)
SCALE2 = SCALE * math.log2(math.e)
MASKED = -1e30
DELTA_ROWS = 16
MIB = 1024 * 1024
NEAR = 4
BLOCKS = 10


def send(value, steps):
    count = lax.axis_size("seq")
    return lax.ppermute(value, "seq", [(i, (i + steps) % count) for i in range(count)])


def swap_pair(value):
    count = lax.axis_size("seq")
    return lax.ppermute(value, "seq", [(i, i ^ 1) for i in range(count)])


def swap_cross(value):
    count = lax.axis_size("seq")
    return lax.ppermute(value, "seq", [(i, (i + (1 if i % 2 else count - 1)) % count) for i in range(count)])


def swap_heads(value):
    return lax.all_to_all(value, "head", split_axis=0, concat_axis=0, tiled=True)


def near_array(shape, dtype):
    return pltpu.VMEM(shape, dtype)


def in_hbm(value):
    return pltpu.with_memory_space_constraint(value, pltpu.HBM)


def near(value):
    return pltpu.with_memory_space_constraint(value, pltpu.VMEM)


SMEM = pl.BlockSpec(memory_space=pltpu.SMEM)
VMEM = pl.BlockSpec(memory_space=pltpu.VMEM)
HBM = pl.BlockSpec(memory_space=pltpu.HBM)


def pack_kernel(parts, q_in, g_in, o_in, k_in, v_in, out, out_ref, q_ref, g_ref, o_ref, k_ref, v_ref, sems):
    rows = q_ref.shape[0]
    owners = out_ref.shape[0]
    width = GROUP * HEAD
    base = 2 * GROUP * rows
    span = owners * width // parts
    wide = []
    for n in range(parts):
        for m, (a, b) in enumerate(((g_in, g_ref), (o_in, o_ref), (q_in, q_ref))):
            cols = pl.ds(n * span, span)
            wide.append(pltpu.make_async_copy(a.at[:, cols], b.at[:, cols], sems.at[3 * n + m]))
    narrow = [
        pltpu.make_async_copy(k_in, k_ref, sems.at[3 * parts]),
        pltpu.make_async_copy(v_in, v_ref, sems.at[3 * parts + 1]),
    ]
    for copy in wide[:3] + narrow + wide[3:]:
        copy.start()
    stores = []
    for n in range(owners):
        if n % (owners // parts) == 0:
            first = 3 * (n // (owners // parts))
            for copy in wide[first : first + 3]:
                copy.wait()
        products = []
        for h in range(GROUP):
            cols = slice(n * width + h * HEAD, n * width + (h + 1) * HEAD)
            grad = g_ref[:, cols]
            out_ref[n, h * rows : (h + 1) * rows, :] = q_ref[:, cols]
            out_ref[n, (GROUP + h) * rows : (GROUP + h + 1) * rows, :] = grad
            products.append(grad.astype(jnp.float32) * o_ref[:, cols].astype(jnp.float32))
        products = jnp.concatenate(products, axis=0)
        lead = products.astype(jnp.bfloat16)
        rest = (products - lead.astype(jnp.float32)).astype(jnp.bfloat16)
        ones = jnp.ones((8, HEAD), jnp.bfloat16)
        across = (((1,), (1,)), ((), ()))
        sums = lax.dot_general(ones, lead, across, preferred_element_type=jnp.float32)
        sums += lax.dot_general(ones, rest, across, preferred_element_type=jnp.float32)
        delta = jnp.concatenate([sums[0:1, :HEAD], sums[0:1, HEAD:]], axis=0)
        high = delta.astype(jnp.bfloat16).astype(jnp.float32)
        spare = jnp.zeros((DELTA_ROWS - GROUP, HEAD), jnp.float32)
        tile = jnp.concatenate([high, delta - high, spare], axis=0)
        out_ref[n, base : base + DELTA_ROWS, :] = tile.astype(jnp.bfloat16)
        if n == 0:
            for copy in narrow:
                copy.wait()
        at = base + DELTA_ROWS
        out_ref[n, at : at + rows, :] = k_ref[:, n * HEAD : (n + 1) * HEAD]
        out_ref[n, at + rows :, :] = v_ref[:, n * HEAD : (n + 1) * HEAD]
        if (n + 1) % (owners // parts) == 0:
            here = pl.ds(n + 1 - owners // parts, owners // parts)
            stores.append(pltpu.make_async_copy(out_ref.at[here], out.at[here], sems.at[3 * parts + 2 + len(stores)]))
            stores[-1].start()
    for copy in stores:
        copy.wait()


def pack(queries, keys, values, grads, outputs, heads):
    rows = queries.shape[0]
    parts = 2
    args = (queries, grads, outputs, keys, values)
    packed = (heads, (2 * GROUP + 2) * rows + DELTA_ROWS, HEAD)
    return pl.pallas_call(
        functools.partial(pack_kernel, parts),
        in_specs=[HBM] * 5,
        out_specs=HBM,
        out_shape=jax.ShapeDtypeStruct(packed, jnp.bfloat16),
        scratch_shapes=[pltpu.VMEM(packed, jnp.bfloat16)]
        + [pltpu.VMEM(x.shape, x.dtype) for x in args]
        + [pltpu.SemaphoreType.DMA((4 * parts + 2,))],
        compiler_params=pltpu.CompilerParams(vmem_limit_bytes=24 * MIB),
        name="pack",
    )(*[in_hbm(x) for x in args])


def plan_kernel(seq_size, mine_ref, order_ref, start_ref, keep_ref, docs_ref):
    def count(b, running):
        running = running + jnp.where(b > 0, start_ref[b], 0)
        docs_ref[b] = running
        return running

    lax.fori_loop(0, order_ref.shape[0], count, jnp.int32(0))
    mine = mine_ref[0]
    odd = lax.rem(mine, 2)
    steps = (0, 1 - 2 * odd, -REACH, REACH, 2 * odd - 1)
    blocks = []
    for step in steps:
        slab = lax.rem(mine + step + seq_size, seq_size)
        blocks += [order_ref[2 * slab], order_ref[2 * slab + 1]]
    docs = [docs_ref[b] for b in blocks]
    for i in range(2):
        for j in range(BLOCKS):
            kept = (blocks[j] <= blocks[i]) & (docs[j] == docs[i])
            keep_ref[i * BLOCKS + j] = kept.astype(jnp.int32)


def plan(mine, block_order, doc_start, seq_size):
    return pl.pallas_call(
        functools.partial(plan_kernel, seq_size),
        in_specs=[SMEM] * 3,
        out_specs=SMEM,
        out_shape=jax.ShapeDtypeStruct((2 * BLOCKS,), jnp.int32),
        scratch_shapes=[pltpu.SMEM((block_order.shape[0],), jnp.int32)],
        name="plan",
    )(mine, block_order, doc_start)


def block_of(ref, j, first, rows):
    per_block = BLK // rows
    tiles = ref[pl.ds(j * per_block, per_block), first : first + rows, :]
    return tiles.reshape(BLK, HEAD)


def near_kernel(
    rows, keep_ref, got_ref, pair_ref, e_own, d_own, e_pair, d_pair, qt_ref, gt_ref, u_ref, stat_ref, kv, scores
):
    per_block = BLK // rows
    chunk = GROUP * rows
    sources = 2 * per_block
    kv_at = 2 * chunk + DELTA_ROWS
    kv[:sources] = got_ref[:, kv_at:, :]
    kv[sources:] = pair_ref[...]

    def score(i, j, diagonal):
        keys = block_of(kv, j, 0, rows)
        for c in range(per_block):
            lanes = slice(c * chunk, (c + 1) * chunk)
            s = jnp.dot(keys, qt_ref[i, :, lanes], preferred_element_type=jnp.float32)
            if diagonal:
                key_at = lax.broadcasted_iota(jnp.int32, (BLK, chunk), 0)
                query_at = c * rows + lax.broadcasted_iota(jnp.int32, (BLK, chunk), 1) % rows
                s = jnp.where(key_at <= query_at, s, MASKED)
            scores[j, :, lanes] = s
            top = jnp.max(s, axis=0, keepdims=True)
            stat_ref[i, 0:1, lanes] = top if diagonal else jnp.maximum(top, stat_ref[i, 0:1, lanes])

    def weigh(i, j, first, own):
        keys_t = block_of(kv, j, 0, rows).T
        values = block_of(kv, j, rows, rows)
        parts = []
        for c in range(per_block):
            lanes = slice(c * chunk, (c + 1) * chunk)
            e = jnp.exp2((scores[j, :, lanes] - stat_ref[i, 0:1, lanes]) * SCALE2)
            total = jnp.sum(e, axis=0, keepdims=True)
            stat_ref[i, 1:2, lanes] = total if first else stat_ref[i, 1:2, lanes] + total
            dprobs = jnp.dot(values, gt_ref[i, :, lanes], preferred_element_type=jnp.float32)
            d = (e * (dprobs - stat_ref[i, 2:3, lanes])).astype(jnp.bfloat16)
            e_ref, d_ref, at = (e_own, d_own, 2 * i + j) if own else (e_pair, d_pair, 2 * i + j - 2)
            e_ref[at, :, lanes] = e.astype(jnp.bfloat16)
            d_ref[at, :, lanes] = d
            parts.append(d)
        u = jnp.dot(keys_t, jnp.concatenate(parts, axis=1), preferred_element_type=jnp.float32)
        u_ref[i] = u if first else u_ref[i] + u

    for i in range(2):
        for c in range(per_block):
            source = i * per_block + c
            lanes = slice(c * chunk, (c + 1) * chunk)
            qt_ref[i, :, lanes] = got_ref[source, :chunk, :].T
            gt_ref[i, :, lanes] = got_ref[source, chunk : 2 * chunk, :].T
            tile = got_ref[source, 2 * chunk : kv_at, :].astype(jnp.float32)
            delta = tile[0:2, :] + tile[2:4, :]
            stat_ref[i, 2:3, c * chunk : c * chunk + HEAD] = delta[0:1, :]
            stat_ref[i, 2:3, c * chunk + HEAD : (c + 1) * chunk] = delta[1:2, :]
        score(i, i, True)

        def visit_scores(j, _):
            @pl.when((keep_ref[i * BLOCKS + j] == 1) & (j != i))
            def _():
                score(i, j, False)

            return 0

        lax.fori_loop(0, NEAR, visit_scores, 0)
        weigh(i, i, True, True)

        @pl.when(keep_ref[i * BLOCKS + 1 - i] == 1)
        def _():
            weigh(i, 1 - i, False, True)

        def visit_weights(j, _):
            @pl.when(keep_ref[i * BLOCKS + j] == 1)
            def _():
                weigh(i, j, False, False)

            return 0

        lax.fori_loop(2, NEAR, visit_weights, 0)


def near_part(keep, got, pair, rows):
    lanes = BLK * GROUP
    return pl.pallas_call(
        functools.partial(near_kernel, rows),
        in_specs=[SMEM, VMEM, VMEM],
        out_specs=[VMEM] * 8,
        out_shape=[
            *[jax.ShapeDtypeStruct((NEAR, BLK, lanes), jnp.bfloat16)] * 4,
            jax.ShapeDtypeStruct((2, HEAD, lanes), jnp.bfloat16),
            jax.ShapeDtypeStruct((2, HEAD, lanes), jnp.bfloat16),
            jax.ShapeDtypeStruct((2, HEAD, lanes), jnp.float32),
            jax.ShapeDtypeStruct((2, 8, lanes), jnp.float32),
        ],
        scratch_shapes=[
            pltpu.VMEM((2 * pair.shape[0],) + pair.shape[1:], jnp.bfloat16),
            pltpu.VMEM((NEAR, BLK, lanes), jnp.float32),
        ],
        compiler_params=pltpu.CompilerParams(vmem_limit_bytes=24 * MIB),
        cost_estimate=pl.CostEstimate(flops=3_000_000_000, bytes_accessed=4_000_000, transcendentals=8_000_000),
        name="near_part",
    )(keep, got, pair)


def far_kernel(
    rows, keep_ref, got_ref, before_ref, after_ref, cross_ref, e_ref, d_ref, qt_ref, gt_ref, u_ref,
    stat_ref, to_before, to_after, to_cross, to_pair, dqt_ref, alpha_ref, kv, scores, acc, stats,
):
    per_block = BLK // rows
    chunk = GROUP * rows
    sources = 2 * per_block
    far_blocks = BLOCKS - NEAR
    kv[:sources] = before_ref[...]
    kv[sources : 2 * sources] = after_ref[...]

    kv[2 * sources :] = cross_ref[...]
    acc[...] = jnp.zeros_like(acc)

    def score(i, j):
        keys = block_of(kv, j, 0, rows)
        for c in range(per_block):
            lanes = slice(c * chunk, (c + 1) * chunk)
            s = jnp.dot(keys, qt_ref[i, :, lanes], preferred_element_type=jnp.float32)
            scores[j, :, lanes] = s
            before = stats[0:1, lanes]
            top = jnp.maximum(jnp.max(s, axis=0, keepdims=True), before)
            stats[0:1, lanes] = top
            stats[1:2, lanes] = stats[1:2, lanes] * jnp.exp2((before - top) * SCALE2) + jnp.sum(
                jnp.exp2((s - top) * SCALE2), axis=0, keepdims=True
            )

    def queries_of(i, first):
        tiles = got_ref[i * per_block : (i + 1) * per_block, first : first + chunk, :]
        return tiles.reshape(per_block * chunk, HEAD)

    def add(j, k, v):
        here = pl.ds(j * per_block, per_block)
        acc[here, :rows, :] += k.reshape(per_block, rows, HEAD)
        acc[here, rows:, :] += v.reshape(per_block, rows, HEAD)

    def gradients(i, j):
        keys_t = block_of(kv, j, 0, rows).T
        values = block_of(kv, j, rows, rows)
        all_p, all_d = [], []
        for c in range(per_block):
            lanes = slice(c * chunk, (c + 1) * chunk)
            probs = jnp.exp2(scores[j, :, lanes] * SCALE2 - stats[2:3, lanes])
            dprobs = jnp.dot(values, gt_ref[i, :, lanes], preferred_element_type=jnp.float32)
            all_d.append((probs * (dprobs - stat_ref[i, 2:3, lanes])).astype(jnp.bfloat16))
            all_p.append(probs.astype(jnp.bfloat16))
        probs = jnp.concatenate(all_p, axis=1)
        dscores = jnp.concatenate(all_d, axis=1)
        v = jnp.dot(probs, queries_of(i, chunk), preferred_element_type=jnp.float32)
        k = jnp.dot(dscores, queries_of(i, 0), preferred_element_type=jnp.float32)
        dqt_ref[i] += jnp.dot(keys_t, dscores, preferred_element_type=jnp.float32)
        add(j, k, v)

    def pair_gradients(i, j):
        p = (e_ref[2 * i + j].astype(jnp.float32) * alpha_ref[i, 0:1, :]).astype(jnp.bfloat16)
        d = (d_ref[2 * i + j].astype(jnp.float32) * alpha_ref[i, 0:1, :]).astype(jnp.bfloat16)
        v = jnp.dot(p, queries_of(i, chunk), preferred_element_type=jnp.float32)
        k = jnp.dot(d, queries_of(i, 0), preferred_element_type=jnp.float32)
        add(far_blocks + j, k, v)

    for i in range(2):
        stats[0:2, :] = stat_ref[i, 0:2, :]

        def visit_scores(j, _):
            @pl.when(keep_ref[i * BLOCKS + NEAR + j] == 1)
            def _():
                score(i, j)

            return 0

        for j in range(far_blocks):
            visit_scores(j, 0)
        lse = stats[0:1, :] * SCALE2 + jnp.log2(stats[1:2, :])
        stats[2:3, :] = lse
        alpha = jnp.exp2(stat_ref[i, 0:1, :] * SCALE2 - lse)
        alpha_ref[i, 0:1, :] = alpha
        dqt_ref[i] = u_ref[i] * alpha

        def visit_gradients(j, _):
            @pl.when(keep_ref[i * BLOCKS + NEAR + j] == 1)
            def _():
                gradients(i, j)

            return 0

        lax.fori_loop(0, far_blocks, visit_gradients, 0)

        def visit_pair(j, _):
            @pl.when(keep_ref[i * BLOCKS + 2 + j] == 1)
            def _():
                pair_gradients(i, j)

            return 0

        lax.fori_loop(0, 2, visit_pair, 0)

    for n, ref in enumerate((to_before, to_after, to_cross, to_pair)):
        here = slice(n * sources, (n + 1) * sources)
        ref[:, :rows, :] = (acc[here, :rows, :] * SCALE).astype(jnp.bfloat16)
        ref[:, rows:, :] = acc[here, rows:, :].astype(jnp.bfloat16)


def far_part(keep, got, before, after, cross, state, rows):
    lanes = BLK * GROUP
    e, d, qt, gt, u, stat = state
    sources, tall, _ = before.shape
    return pl.pallas_call(
        functools.partial(far_kernel, rows),
        in_specs=[SMEM] + [VMEM] * 10,
        out_specs=[VMEM] * 6,
        out_shape=[
            *[jax.ShapeDtypeStruct((sources, tall, HEAD), jnp.bfloat16)] * 4,
            jax.ShapeDtypeStruct((2, HEAD, lanes), jnp.float32),
            jax.ShapeDtypeStruct((2, 8, lanes), jnp.float32),
        ],
        scratch_shapes=[
            pltpu.VMEM((3 * sources, tall, HEAD), jnp.bfloat16),
            pltpu.VMEM((BLOCKS - NEAR, BLK, lanes), jnp.float32),
            pltpu.VMEM((4 * sources, tall, HEAD), jnp.float32),
            pltpu.VMEM((8, lanes), jnp.float32),
        ],
        compiler_params=pltpu.CompilerParams(vmem_limit_bytes=24 * MIB),
        cost_estimate=pl.CostEstimate(flops=3_000_000_000, bytes_accessed=4_000_000, transcendentals=8_000_000),
        name="far_part",
    )(keep, got, before, after, cross, e, d, qt, gt, u, stat)


def own_kernel(rows, keep_ref, got_ref, e_ref, d_ref, dqt_ref, alpha_ref, own_ref, out_ref):
    per_block = BLK // rows
    chunk = GROUP * rows

    def add(i, j):
        p = (e_ref[2 * i + j].astype(jnp.float32) * alpha_ref[i, 0:1, :]).astype(jnp.bfloat16)
        d = (d_ref[2 * i + j].astype(jnp.float32) * alpha_ref[i, 0:1, :]).astype(jnp.bfloat16)
        tiles = got_ref[i * per_block : (i + 1) * per_block, : 2 * chunk, :]
        q = tiles[:, :chunk, :].reshape(per_block * chunk, HEAD)
        g = tiles[:, chunk:, :].reshape(per_block * chunk, HEAD)
        v = jnp.dot(p, g, preferred_element_type=jnp.float32)
        k = jnp.dot(d, q, preferred_element_type=jnp.float32) * SCALE
        here = slice(j * per_block, (j + 1) * per_block)
        own_ref[here, :rows, :] += k.reshape(per_block, rows, HEAD)
        own_ref[here, rows:, :] += v.reshape(per_block, rows, HEAD)

    own_ref[...] = jnp.zeros_like(own_ref)
    for i in range(2):
        add(i, i)
        pl.when(keep_ref[i * BLOCKS + 1 - i] == 1)(functools.partial(add, i, 1 - i))
        for c in range(per_block):
            dq = (dqt_ref[i, :, c * chunk : (c + 1) * chunk] * SCALE).T
            out_ref[i * per_block + c, :chunk, :] = dq.astype(jnp.bfloat16)


def own_part(keep, got, e, d, dqt, alpha, rows):
    return pl.pallas_call(
        functools.partial(own_kernel, rows),
        in_specs=[SMEM] + [VMEM] * 5,
        out_specs=[VMEM] * 2,
        out_shape=[
            jax.ShapeDtypeStruct((got.shape[0], 2 * rows, HEAD), jnp.float32),
            jax.ShapeDtypeStruct((got.shape[0], (GROUP + 2) * rows, HEAD), jnp.bfloat16),
        ],
        compiler_params=pltpu.CompilerParams(vmem_limit_bytes=16 * MIB),
        cost_estimate=pl.CostEstimate(flops=1_000_000_000, bytes_accessed=4_000_000, transcendentals=0),
        name="own_part",
    )(keep, got, e, d, dqt, alpha)


def unpack_kernel(rows, parts, got_ref, q_out, k_out, v_out, q_ref, k_ref, v_ref, sems):
    owners = got_ref.shape[0]
    width = GROUP * HEAD
    copies = []
    for n in range(owners):
        for h in range(GROUP):
            q_ref[:, n * width + h * HEAD : n * width + (h + 1) * HEAD] = got_ref[n, h * rows : (h + 1) * rows, :]
        k_ref[:, n * HEAD : (n + 1) * HEAD] = got_ref[n, GROUP * rows : (GROUP + 1) * rows, :]
        v_ref[:, n * HEAD : (n + 1) * HEAD] = got_ref[n, (GROUP + 1) * rows :, :]
        if (n + 1) % (owners // parts) == 0:
            span = owners * width // parts
            cols = pl.ds((n + 1) * width - span, span)
            copies.append(pltpu.make_async_copy(q_ref.at[:, cols], q_out.at[:, cols], sems.at[len(copies)]))
            copies[-1].start()
    copies.append(pltpu.make_async_copy(k_ref, k_out, sems.at[parts]))
    copies.append(pltpu.make_async_copy(v_ref, v_out, sems.at[parts + 1]))
    copies[-2].start()
    copies[-1].start()
    for copy in copies:
        copy.wait()


def unpack(got, rows):
    heads = got.shape[0]
    parts = 4
    shapes = [(rows, heads * GROUP * HEAD), (rows, heads * HEAD), (rows, heads * HEAD)]
    return pl.pallas_call(
        functools.partial(unpack_kernel, rows, parts),
        in_specs=[VMEM],
        out_specs=[HBM] * 3,
        out_shape=[jax.ShapeDtypeStruct(x, jnp.bfloat16) for x in shapes],
        scratch_shapes=[pltpu.VMEM(x, jnp.bfloat16) for x in shapes] + [pltpu.SemaphoreType.DMA((parts + 2,))],
        compiler_params=pltpu.CompilerParams(vmem_limit_bytes=16 * MIB),
        name="unpack",
    )(got)


def local(queries, keys, values, output_gradient, outputs, block_order, doc_start):
    heads = lax.axis_size("head")
    seq_size = lax.axis_size("seq")
    rows = queries.shape[0]
    place = lax.axis_index("seq").astype(jnp.int32)
    keep = plan(place.reshape(1), block_order, doc_start, seq_size)
    got = swap_heads(pack(queries, keys, values, output_gradient, outputs, heads))
    kv = got[:, 2 * GROUP * rows + DELTA_ROWS :, :]
    kv, keep = lax.optimization_barrier((kv, keep))
    after, before = send(kv, -REACH), send(kv, REACH)
    pair = swap_pair(kv)
    state = near_part(keep, got, pair, rows)
    e_own, d_own, *state = state
    after, before, *state = lax.optimization_barrier((after, before, *state))
    cross = swap_pair(jnp.where(lax.rem(place, 2) == 1, before, after))
    *sums, dqt, alpha = far_part(
        keep, got, before, after, cross, state, rows
    )
    to_before, to_after, to_cross, to_pair = sums
    back = (send(to_before, -REACH), send(to_after, REACH), swap_cross(to_cross), swap_pair(to_pair))
    total, out = own_part(keep, got, e_own, d_own, dqt, alpha, rows)
    for part in back:
        total = total + part.astype(jnp.float32)
    out = lax.dynamic_update_slice(out, total.astype(jnp.bfloat16), (0, GROUP * rows, 0))
    return tuple(unpack(swap_heads(out), rows))


def solution(mesh):
    rows = P(("seq", "head"), None)
    return jax.shard_map(
        local,
        mesh=mesh,
        in_specs=(rows, rows, rows, rows, rows, P(), P()),
        out_specs=(rows, rows, rows),
        check_vma=False,
    )
```
